128 devices in a mesh: row: 8 (over y, core), col: 16 (over x, z).
Axes of the slice: x: 4, y: 4, z: 4, core: 2. Of those that a mesh axis runs over, the one named last changes fastest.
Arguments:
- hess: bfloat16 [10, 8, 256, 5, 16, 256], P(None, 'row', None, None, 'col'), may hold values from -6 to 6
- coupling: float32 [128, 256, 2, 256], P(('row', 'col')), may hold values from -6 to 6
- dest_row: int32 [128, 256, 1], P(('row', 'col')), may hold values from 0 to 7, as said below
- local_row: int32 [128, 256], P(('row', 'col')), may hold values from 256 to 2559
- live: int32 [128], P(('row', 'col')), may hold values from 1 to 256, 24576 in all
- pattern: int32 [80, 80], replicated, may hold values 0 or 1
Outputs:
- factor: float32 [10, 8, 256, 5, 16, 256], P(None, 'row', None, None, 'col')
The draws below stay inside these ranges and needn't reach their ends.
Inputs may be any that keep to these rules, and one draw needn't show every extreme that they name: `dest_row`: among one owner's 256 slots, used or not, one grid row is named exactly 64 times and no grid row more than 64 times. The first live[d] slots of owner d are used; the counts sum to 24576 and one owner uses all 256.
All inputs are finite; a program needn't handle non-finite values. No bound on the sum of `live` on one device may be relied on, other than what follows from the above.
Results may differ from the reference program's by a relative error of at most 0.0003.
Values sent between devices are 32-bit elements; how exact they have to be, the bound alone decides.
A program may use at most 192 MiB of HBM per device.

```python
import math
import jax
import jax.numpy as jnp
import numpy as np
from jax import lax

B = 256
RB_DEV = 10
SLOTS = 256
NBLK = 80
CB_DEV = 5
OWNERS = 128
CAP = 64
N_ROW = 8
N_COL = 16


def draw_hess(key, part):
    shape = (RB_DEV, N_ROW, B, CB_DEV, N_COL, B)
    base_key = jax.random.fold_in(key, 11)
    noise = jax.random.normal(base_key, shape, jnp.float32)
    values = 1.5 + 0.5 * noise
    values = jnp.clip(values, -6.0, 6.0)
    return values.astype(jnp.bfloat16)


def owner_routes(owner_key):
    keys = jax.random.split(owner_key, 4)
    first_pick = jax.random.randint(keys[0], (), 0, N_ROW, dtype=jnp.int32)
    second_pick = jax.random.randint(keys[1], (), 0, N_ROW, dtype=jnp.int32)
    heavy = jnp.minimum(first_pick, second_pick)
    others = jnp.arange((N_ROW - 1) * CAP, dtype=jnp.int32) // CAP
    others = others + (others >= heavy).astype(jnp.int32)
    shuffled = jax.random.permutation(keys[2], others)
    chosen = shuffled[:SLOTS - CAP]
    combined = jnp.concatenate([jnp.zeros((CAP,), jnp.int32) + heavy, chosen], 0)
    return jax.random.permutation(keys[3], combined)


def draw_dest_row(key, part):
    owner_keys = jax.random.split(jax.random.fold_in(key, 7), OWNERS)
    routes_all = jax.vmap(owner_routes)(owner_keys)
    return routes_all[:, :, None].astype(jnp.int32)


def set_ends(values, stream_key, low, largest):
    longest = values.shape.index(max(values.shape))
    spots = []
    for shift in (0, 1):
        where = [jax.random.randint(jax.random.fold_in(stream_key, axis), (), 0, length) for axis, length in enumerate(values.shape)]
        where[longest] = (where[longest] + shift) % values.shape[longest]
        spots.append(tuple(where))
    return values.at[spots[0]].set(low).at[spots[1]].set(largest)


def block_levels(own_key, extent, cuts, least, largest):
    gain, own = 1.0, jax.random.fold_in(own_key, 6)
    for position, blocks in cuts:
        steps = jnp.exp(jax.random.uniform(jax.random.fold_in(own, position), (blocks,), jnp.float32, least / len(cuts), largest / len(cuts)))
        gain = gain * jnp.repeat(steps, extent[position] // blocks).reshape([-1 if axis == position else 1 for axis in range(len(extent))])
    return gain


def split_up(count, total, most, slope):
    weights = [(1 << 20) // math.isqrt(grade ** slope) + 1 for grade in range(2, count + 1)]
    spare, counts = total - most - (count - 1), [1] * (count - 1)
    while spare > 0:
        candidates = [i for i in range(count - 1) if counts[i] < most]
        pool, remaining = sum([weights[i] for i in candidates]), spare
        for i in candidates:
            more = min(most - counts[i], max(1, remaining * weights[i] // pool), spare)
            counts[i] = counts[i] + more
            spare = spare - more
    return np.array([most] + counts)


def ragged_sizes(stream_key, number_of, total, reach, slope):
    if number_of == 2:
        one = jax.random.randint(stream_key, (), max(1, total - reach), min(reach, total - 1) + 1)
        return jnp.stack([one, total - one])
    lengths = jnp.asarray(split_up(number_of, total, reach, slope), jnp.int32)
    twos = (number_of - 1) // 2
    donor, sink = lengths[1:1 + 2 * twos:2], lengths[2:2 + 2 * twos:2]
    slack = jnp.minimum(donor - 1, reach - sink)
    passed = jax.random.randint(jax.random.fold_in(stream_key, 1), (twos,), 0, 1 << 20) % (slack + 1)
    lengths = lengths.at[1:1 + 2 * twos:2].set(donor - passed).at[2:2 + 2 * twos:2].set(sink + passed)
    return lengths[jax.random.permutation(jax.random.fold_in(stream_key, 2), number_of)]


def gaussian(key, extent, width, most, pieces=(), kind=jnp.bfloat16):
    gain = block_levels(key, extent, pieces, -0.22, 0.18) if pieces else 1.0
    values = jax.random.normal(key, extent, jnp.float32) * width * gain
    return jnp.minimum(jnp.maximum(values, -most), most).astype(kind)


def setup_inputs(seed: int = 0) -> dict:
    key_of = jax.random.split(jax.random.key(seed), 7)
    return {
        "hess": draw_hess(jax.random.fold_in(key_of[6], 71), 0),
        "coupling": gaussian(key_of[1], (OWNERS, SLOTS, 2, B), 1.0, 6.0, ((0, 128),), jnp.float32),
        "dest_row": draw_dest_row(jax.random.fold_in(key_of[6], 71), 0),
        "local_row": set_ends(jax.random.randint(key_of[3], (OWNERS, SLOTS), B, RB_DEV * B), jax.random.fold_in(key_of[3], 1), B, (RB_DEV * B) - 1).astype(jnp.int32),
        "live": ragged_sizes(key_of[4], OWNERS, OWNERS * SLOTS * 3 // 4, SLOTS, 2).astype(jnp.int32),
        "pattern": set_ends((jax.random.randint(key_of[5], (NBLK, NBLK), 0, 2) < 1).astype(jnp.int32), jax.random.fold_in(key_of[5], 1), 0, 1),
    }


def symmetric(block):
    return jnp.tril(block) + jnp.swapaxes(jnp.tril(block, -1), -1, -2)

def right_solve(rows, lower_factor):
    return jax.scipy.linalg.solve_triangular(lower_factor, rows.T, lower=True).T

def leading(block00, block10, block11, link):
    size = block00.shape[0]
    first = symmetric(block00)
    second = symmetric(block11)
    coupled = link * block10
    whole = jnp.concatenate([jnp.concatenate([first, coupled.T], 1), jnp.concatenate([coupled, second], 1)], 0)
    ident = jnp.eye(2 * size, dtype=whole.dtype)
    spread = jnp.sum(jnp.abs(whole), axis=1) - jnp.abs(jnp.diagonal(whole))
    whole = whole * (1.0 - ident) + ident * (1.0 + spread)[:, None]
    factor00 = jnp.linalg.cholesky(whole[:size, :size])
    factor10 = right_solve(whole[size:, :size], factor00)
    reduced = whole[size:, size:] - jnp.dot(factor10, factor10.T, precision=lax.Precision.HIGHEST)
    factor11 = jnp.linalg.cholesky(reduced)
    return (factor00, factor10, factor11)

def reference(hess, coupling, dest_row, local_row, live, pattern):
    order = NBLK * B
    matrix = hess.astype(jnp.float32).reshape(order, order)
    blocks = matrix.reshape(NBLK, B, NBLK, B)
    mask = pattern.astype(jnp.float32)
    slot_ids = jnp.arange(SLOTS, dtype=jnp.int32)
    active = slot_ids[None, :] < live[:, None]
    target = (local_row // B * N_ROW + dest_row[:, :, 0]) * B + local_row % B
    moved = jnp.where(active[:, :, None, None], coupling, 0.0)
    extra = jnp.zeros((order, 2, B), jnp.float32).at[target.reshape(-1)].add(moved.reshape(-1, 2, B))
    panel = jnp.stack([matrix[:, :B], matrix[:, B:2 * B]], 1) + extra
    rowmask = jnp.repeat(mask[:, :2], B, axis=0)
    panel = panel * rowmask[:, :, None]
    f00, f10, f11 = leading(blocks[0, :, 0], blocks[1, :, 0], blocks[1, :, 1], mask[1, 0])
    first = right_solve(panel[:, 0], f00)
    second = right_solve(panel[:, 1] - jnp.dot(first, f10.T, precision=lax.Precision.HIGHEST), f11)
    empty = jnp.zeros((B, B), jnp.float32)
    first = jnp.concatenate([f00, f10, first[2 * B:]], 0)
    second = jnp.concatenate([empty, f11, second[2 * B:]], 0)
    factor = jnp.concatenate([first, second], 1)
    index = jnp.arange(NBLK, dtype=jnp.int32)
    filler = jnp.zeros((NBLK - 2, B, B), jnp.float32)

    def row_block(i):
        rows = lax.dynamic_slice_in_dim(matrix, i * B, B, 0)
        left = lax.dynamic_slice_in_dim(factor, i * B, B, 0)
        update = jnp.dot(left, factor.T, precision=lax.Precision.HIGHEST)
        tiles = jnp.swapaxes(rows.reshape(B, NBLK, B), 0, 1)
        sym = symmetric(tiles)
        links = lax.dynamic_index_in_dim(mask, i, 0, keepdims=False)
        base = jnp.where((index == i)[:, None, None], sym, jnp.where((index < i)[:, None, None], links[:, None, None] * tiles, 0.0))
        trail = base - jnp.swapaxes(update.reshape(B, NBLK, B), 0, 1)
        panel_part = jnp.concatenate([jnp.swapaxes(left.reshape(B, 2, B), 0, 1), filler], 0)
        result = jnp.where((index < 2)[:, None, None], panel_part, jnp.where((index <= i)[:, None, None], trail, 0.0))
        return jnp.swapaxes(result, 0, 1).reshape(B, order)
    full = lax.map(row_block, index).reshape(order, order)
    return full.reshape(RB_DEV, N_ROW, B, CB_DEV, N_COL, B)
```

```python
import jax
import jax.numpy as jnp
from jax import lax
from jax.experimental import pallas as pl
from jax.experimental.pallas import tpu as pltpu
from jax.sharding import PartitionSpec as P

F32 = jnp.float32
BF = jnp.bfloat16
MESH = pl.DeviceIdType.MESH
NR, NC, NX, NZ = 8, 16, 4, 4


def dotg(a, b, ca, cb, precision=lax.Precision.HIGHEST):
    return lax.dot_general(
        a, b, (((ca,), (cb,)), ((), ())), precision=precision, preferred_element_type=F32
    )


def dot1(a, b, ca, cb):
    return lax.dot_general(a, b, (((ca,), (cb,)), ((), ())), preferred_element_type=F32)


def split(x):
    hi = x.astype(BF)
    return hi, (x - hi.astype(F32)).astype(BF)


def iota(shape, dim):
    return lax.broadcasted_iota(jnp.int32, shape, dim)


def sym_block(x):
    n = x.shape[0]
    return jnp.where(iota((n, n), 0) >= iota((n, n), 1), x, x.T)


def build_g(h00, h10, h11, link, g_ref):
    g_ref[0:256, 0:256] = sym_block(h00)
    g_ref[256:512, 256:512] = sym_block(h11)
    x = h10 * link
    g_ref[256:512, 0:256] = x
    g_ref[0:256, 256:512] = x.T
    for i in range(4):
        rows = slice(i * 128, (i + 1) * 128)
        g = g_ref[rows, :]
        on = iota((128, 512), 0) + i * 128 == iota((128, 512), 1)
        s = jnp.sum(jnp.where(on, 0.0, jnp.abs(g)), axis=1, keepdims=True) + 1.0
        g_ref[rows, :] = jnp.where(on, s, g)


def panels(s_ref, lo, hi):
    lane = iota((8, 128), 1)
    sub = iota((8, 1), 0)

    def body(b, carry):
        base = pl.multiple_of(b * 8, 8)
        rows = s_ref[pl.ds(base, 8), :]
        ra = rows[:, :128]
        cs = [
            jnp.sum(jnp.where(lane == base + j, ra, 0.0), axis=1, keepdims=True)
            for j in range(8)
        ]
        invd = jnp.zeros((8, 1), F32)
        for j in range(8):
            inv = 1.0 / cs[j][j : j + 1, :]
            m = jnp.where(sub > j, cs[j] * inv, 0.0)
            invd = jnp.where(sub == j, inv, invd)
            rows = rows - m * rows[j : j + 1, :]
            for k in range(j + 1, 8):
                cs[k] = cs[k] - m * cs[k][j : j + 1, :]
        s_ref[pl.ds(base, 8), :] = rows
        um = jnp.where(lane >= base + 8, rows[:, :128], 0.0)
        s_ref[...] = s_ref[...] - dotg(um, rows * invd, 0, 0)
        return carry

    lax.fori_loop(lo, hi, body, 0)


def diag_begin(k, g_ref, s_ref):
    o = k * 128
    s_ref[:, 0:128] = g_ref[o : o + 128, o : o + 128]
    s_ref[:, 128:256] = jnp.where(iota((128, 128), 0) == iota((128, 128), 1), 1.0, 0.0)


def diag_end(k, g_ref, s_ref, l_ref, v_ref):
    o, e = k * 128, k * 128 + 128
    r, c = iota((128, 128), 0), iota((128, 128), 1)
    u = s_ref[:, 0:128]
    s = lax.rsqrt(jnp.sum(jnp.where(r == c, u, 0.0), axis=1, keepdims=True))
    l_ref[o:e, o:e] = jnp.where(r <= c, u * s, 0.0).T
    v = s_ref[:, 128:256] * s
    v_ref[o:e, o:e] = v
    if e < 512:
        lp = dotg(g_ref[e:512, o:e], v, 1, 1)
        l_ref[e:512, o:e] = lp
        l_ref[o:e, e:512] = jnp.zeros((128, 512 - e), F32)
        v_ref[o:e, e:512] = jnp.zeros((128, 512 - e), F32)
        g_ref[e:512, e:512] = g_ref[e:512, e:512] - dotg(lp, lp, 1, 1)
    if o > 0:
        t = dotg(l_ref[o:e, 0:o], v_ref[0:o, 0:o], 1, 0)
        v_ref[o:e, 0:o] = -dotg(v, t, 1, 0)


def move_kernel(
    live_ref, link_ref, dest_ref, lrow_ref, coup_ref, hcol_ref,
    oa_ref, ob_ref, ja_ref, jb_ref, l_ref, v_ref,
    pack_s, pack_r, rows_hi, rows_lo, pv, pv_src, pa, pb, ra1, rb1, ra2, rb2, own_a, own_b,
    g_ref, s_ref,
    a2a_s, a2a_r, p1_s, p1_r, p2_s, p2_r, p3_s, p3_r, rs_s, rs_r, ag_s, ag_r, y_s, y_r, loc,
):
    r = lax.axis_index("row")
    c = lax.axis_index("col")
    x, z = c // NZ, c % NZ

    def copy(src, dst, ss, rs, dev):
        return pltpu.make_async_remote_copy(
            src_ref=src, dst_ref=dst, send_sem=ss, recv_sem=rs, device_id=dev,
            device_id_type=MESH,
        )

    barrier = pltpu.get_barrier_semaphore()
    for d in range(1, NR):
        pl.semaphore_signal(barrier, 1, device_id=((r + d) % NR, c), device_id_type=MESH)
    for d in range(1, NC):
        pl.semaphore_signal(barrier, 1, device_id=(r, (c + d) % NC), device_id_type=MESH)

    pv_src[...] = hcol_ref[0].astype(F32).reshape(NC, 16, 256)

    lane = iota((1, 256), 1)
    active = lane < live_ref[0]
    dest = dest_ref[...]
    hits = jnp.where((iota((NR, 256), 0) == dest) & active, 1.0, 0.0)
    before = jnp.where(iota((256, 256), 0) <= iota((256, 256), 1), 1.0, 0.0).astype(BF)
    cum = dot1(hits.astype(BF), before, 1, 0)
    rank = jnp.sum(hits * cum, axis=0, keepdims=True).astype(jnp.int32) - 1
    place = jnp.where(active, dest * 64 + rank, -1)
    pick = jnp.where(iota((512, 256), 0) == place, 1.0, 0.0).astype(BF)
    c_hi, c_lo = split(coup_ref[...])
    packed = dot1(pick, c_hi, 1, 0) + dot1(pick, c_lo, 1, 0)
    pack_s[:, 0:64, :] = packed.reshape(NR, 64, 512)
    lr = lrow_ref[...]
    spot = jnp.where(iota((512, 256), 0) == rank + r * 64, 1.0, 0.0).astype(BF)
    lab_hi = (hits * (lr // 256).astype(F32)).astype(BF)
    lab_lo = (hits * (lr % 256).astype(F32)).astype(BF)
    labels = (
        dot1(lab_hi, spot, 1, 1) * 256.0
        + dot1(lab_lo, spot, 1, 1)
        + dot1(hits.astype(BF), spot, 1, 1)
    )
    for g in range(NR):
        pack_s[g, 64:72, :] = jnp.broadcast_to(labels[g : g + 1, :], (8, 512))

    pl.semaphore_wait(barrier, NR - 1 + NC - 1)

    sources = ((0, 0), (1, 0), (1, 1))

    def p1(b, d):
        to = (sources[b][1] + d) % NC
        return copy(pv_src.at[to], pv.at[b, to], p1_s.at[b, d], p1_r.at[b], (sources[b][0], to))

    for b, (sr, sc) in enumerate(sources):

        @pl.when((r == sr) & (c == sc))
        def _():
            for d in range(1, NC):
                p1(b, d).start()
            pv[b, sc] = pv_src[sc]

    def a2a(d):
        to = (r + d) % NR
        return copy(pack_s.at[to], pack_r.at[r], a2a_s.at[d], a2a_r.at[d], (to, c))

    for d in range(1, NR):
        a2a(d).start()
    pack_r[r] = pack_s[r]

    for b, (sr, sc) in enumerate(sources):

        @pl.when((r == sr) & (c != sc))
        def _():
            p1(b, 1).wait_recv()

    def p2(k, d):
        blocks = pl.ds(0, 1) if k == 0 else pl.ds(1, 2)
        to = (k + d) % NR
        part = pv.at[blocks, c]
        return copy(part, part, p2_s.at[k, d], p2_r.at[k], (to, c))

    for k in (0, 1):

        @pl.when(r == k)
        def _():
            for d in range(1, NR):
                p2(k, d).start()

    for k in (0, 1):

        @pl.when(r != k)
        def _():
            p2(k, 1).wait_recv()

    def p3(d):
        part = pv.at[:, c]
        return copy(part, part, p3_s.at[d], p3_r.at[d], (r, (c + d) % NC))

    for d in range(1, NC):
        p3(d).start()

    for d in range(1, NR):
        a2a(d).wait_recv()
    lab = jnp.zeros((8, 512), F32)
    for g in range(NR):
        lab = lab + pack_r[g, 64:72, :]
        hi, lo = split(pack_r[g, 0:64, :])
        rows_hi[g * 64 : (g + 1) * 64, :] = hi
        rows_lo[g * 64 : (g + 1) * 64, :] = lo
    lab = lab[0:1, :].astype(jnp.int32) - 1
    first = jnp.where(c == 0, 1.0, 0.0)
    second = jnp.where(c == 1, 1.0, 0.0)
    for p in (0, 1):

        def fill(t2, carry):
            t = t2 * 2 + p
            pick = jnp.where(iota((256, 512), 0) + t * 256 == lab, 1.0, 0.0).astype(BF)
            got = dot1(pick, rows_hi[...], 1, 0) + dot1(pick, rows_lo[...], 1, 0)
            h = hcol_ref[t].astype(F32)
            pa[p, t2] = (got[:, 0:256] + h * first).reshape(NX, NZ, 16, 256)
            pb[p, t2] = (got[:, 256:512] + h * second).reshape(NX, NZ, 16, 256)
            return carry

        lax.fori_loop(0, 5, fill, 0)

    def along_x(n):
        return (r, (n % NX) * NZ + z)

    def along_z(n):
        return (r, x * NZ + n % NZ)

    halves = (
        (
            (x, along_x, lambda n, p: pa.at[p, :, n % 4], ra1),
            (z, along_z, lambda n, p: pa.at[p, :, x, n % 4], ra2),
            (z, along_z, lambda n, p: oa_ref.at[p, :, x, n % 4]),
            (x, along_x, lambda n, p: oa_ref.at[p, :, n % 4]),
        ),
        (
            (z, along_z, lambda n, p: pb.at[p, :, :, n % 4], rb1),
            (x, along_x, lambda n, p: pb.at[p, :, n % 4, z], rb2),
            (x, along_x, lambda n, p: ob_ref.at[p, :, n % 4, z]),
            (z, along_z, lambda n, p: ob_ref.at[p, :, :, n % 4]),
        ),
    )

    def rs(half, phase, m):
        n, dev, unit, buf = halves[half][phase]
        src, to = (
            (unit(n + 2, 0), n + 1),
            (unit(n + 1, 1), n + 1),
            (unit(n + 1, 0), n + 1),
            (unit(n + 2, 1), n + 3),
            (unit(n + 3, 0), n + 3),
            (unit(n + 3, 1), n + 3),
        )[m]
        return copy(
            src, buf.at[m], rs_s.at[half, phase, m], rs_r.at[half, phase, m], dev(to)
        )

    def rs_start(half, phase):
        for m in (0, 3, 1, 4):
            rs(half, phase, m).start()

    def rs_middle(half, phase):
        n, dev, unit, buf = halves[half][phase]
        for m_in, m_out, to, p in ((0, 2, n + 1, 0), (3, 5, n + 3, 1)):
            rs(half, phase, m_in).wait_recv()
            ref = unit(to, p)
            ref[...] = ref[...] + buf[m_in]
            rs(half, phase, m_out).start()

    def rs_end(half, phase):
        n, dev, unit, buf = halves[half][phase]
        for m in (1, 4, 2, 5):
            rs(half, phase, m).wait_recv()
        for p, (m1, m2) in enumerate(((2, 4), (1, 5))):
            ref = unit(n, p)
            ref[...] = ref[...] + (buf[m1] + buf[m2])

    def rs_drain(half, phase):
        for m in range(6):
            rs(half, phase, m).wait_send()

    def ag(half, phase, m):
        n, dev, unit = halves[half][2 + phase]
        src, to = (
            (unit(n, 0), n + 1),
            (unit(n, 1), n + 1),
            (unit(n, 1), n + 3),
            (unit(n, 0), n + 3),
            (unit(n + 3, 0), n + 1),
            (unit(n + 1, 1), n + 3),
        )[m]
        return copy(src, src, ag_s.at[half, phase, m], ag_r.at[half, phase, m], dev(to))

    def ag_start(half, phase):
        for m in (0, 2, 1, 3):
            ag(half, phase, m).start()

    def ag_forward(half, phase):
        for m_in, m_out in ((0, 4), (2, 5)):
            ag(half, phase, m_in).wait_recv()
            ag(half, phase, m_out).start()

    def ag_wait(half, phase, ms):
        for m in ms:
            ag(half, phase, m).wait_recv()

    def ag_drain(half, phase):
        for m in range(6):
            ag(half, phase, m).wait_send()

    y, ys = r // 2, (c % NR) // 2
    chain = r % 2 == c % 2
    par = c // NR
    hop = ((y - ys + 4) % 4, (ys - y + 4) % 4)

    def y_refs(half, n):
        if half == 0:
            return oa_ref.at[par, :, n % 4], ja_ref.at[:, n % 4]
        return ob_ref.at[par, :, :, n % 4], jb_ref.at[:, :, n % 4]

    def y_copy(half, n, k, i, from_o):
        o, j = y_refs(half, n)
        step = 2 if half == 0 else 6
        to = ((r + step) % NR, c) if i == 0 else (r + 1 - 2 * (r % 2), c)
        return copy(o if from_o else j, j, y_s.at[half, k, i], y_r.at[half, k], to)

    def y_local(half, n, k):
        o, j = y_refs(half, n)
        return pltpu.make_async_copy(o, j, loc.at[half, k])

    def y_source(half, n, k):
        @pl.when(chain & (hop[half] == 0))
        def _():
            y_copy(half, n, k, 0, True).start()
            y_copy(half, n, k, 1, True).start()
            y_local(half, n, k).start()

    def y_chain(half, n, k):
        @pl.when(jnp.logical_not(chain) | (hop[half] != 0))
        def _():
            y_copy(half, n, k, 0, False).wait_recv()

        @pl.when(chain & (hop[half] > 0))
        def _():
            @pl.when(hop[half] < 3)
            def _():
                y_copy(half, n, k, 0, False).start()

            y_copy(half, n, k, 1, False).start()

    def y_drain(half, n, k):
        @pl.when(chain & (hop[half] == 0))
        def _():
            y_local(half, n, k).wait()

        @pl.when(chain & (hop[half] < 3))
        def _():
            y_copy(half, n, k, 0, False).wait_send()

        @pl.when(chain)
        def _():
            y_copy(half, n, k, 1, False).wait_send()

    def factor(lo, hi):
        for q in range(lo, hi):
            k, part = q // 4, q % 4
            if q == 0:
                for d in range(1, NC):
                    p3(d).wait_recv()
                build_g(
                    pv[0].reshape(256, 256), pv[1].reshape(256, 256), pv[2].reshape(256, 256),
                    link_ref[0].astype(F32), g_ref,
                )
            if part == 0:
                diag_begin(k, g_ref, s_ref)
            panels(s_ref, part * 4, part * 4 + 4)
            if part == 3:
                diag_end(k, g_ref, s_ref, l_ref, v_ref)

    both = (0, 1)
    for h in both:
        rs_start(h, 0)
    factor(0, 3)
    for h in both:
        rs_middle(h, 0)
    factor(3, 6)
    for h in both:
        rs_end(h, 0)
        rs_start(h, 1)
    factor(6, 7)
    for h in both:
        rs_middle(h, 1)
    factor(7, 8)
    for h, own, o_ref, p_ref in ((0, own_a, oa_ref, pa), (1, own_b, ob_ref, pb)):
        rs_end(h, 1)
        keep = pltpu.make_async_copy(p_ref.at[:, :, x, z], o_ref.at[:, :, x, z], loc.at[h, 4])
        keep.start()
        keep.wait()
        ag_start(h, 0)
    factor(8, 9)
    for h in both:
        ag_forward(h, 0)
    factor(9, 10)
    for h in both:
        ag_wait(h, 0, (1, 3, 4, 5))
        ag_start(h, 1)
        y_source(h, (x, z)[h], 0)
    factor(10, 12)
    for h in both:
        ag_forward(h, 1)
    for h in both:
        y_chain(h, (x, z)[h], 0)
    factor(12, 14)
    for h in both:
        n = (x, z)[h]
        ag_wait(h, 1, (1,))
        y_source(h, n + 3, 1)
        ag_wait(h, 1, (3,))
        y_source(h, n + 1, 2)
    factor(14, 16)
    for h in both:
        n = (x, z)[h]
        y_chain(h, n + 3, 1)
        y_chain(h, n + 1, 2)
    for h in both:
        n = (x, z)[h]
        ag_wait(h, 1, (4, 5))
        y_source(h, n + 2, 3)
    for h in both:
        y_chain(h, (x, z)[h] + 2, 3)

    for h in both:
        n = (x, z)[h]
        for k, m in enumerate((n, n + 3, n + 1, n + 2)):
            y_drain(h, m, k)
        for phase in (0, 1):
            rs_drain(h, phase)
            ag_drain(h, phase)
    for d in range(1, NR):
        a2a(d).wait_send()
    for b, (sr, sc) in enumerate(sources):

        @pl.when((r == sr) & (c == sc))
        def _():
            for d in range(1, NC):
                p1(b, d).wait_send()

    for k in (0, 1):

        @pl.when(r == k)
        def _():
            for d in range(1, NR):
                p2(k, d).wait_send()

    for d in range(1, NC):
        p3(d).wait_send()


def move(live, link, dest, lrow, coup, hcol):
    vm = pl.BlockSpec(memory_space=pltpu.VMEM)
    sm = pl.BlockSpec(memory_space=pltpu.SMEM)
    hb = pl.BlockSpec(memory_space=pl.ANY)
    dma = pltpu.SemaphoreType.DMA
    half = jax.ShapeDtypeStruct((2, 5, NX, NZ, 16, 256), F32)
    cols = jax.ShapeDtypeStruct((5, NX, NZ, 16, 256), F32)
    square = jax.ShapeDtypeStruct((512, 512), F32)
    return pl.pallas_call(
        move_kernel,
        out_shape=(half, half, cols, cols, square, square),
        in_specs=[sm, sm, vm, vm, vm, vm],
        out_specs=[hb, hb, hb, hb, vm, vm],
        scratch_shapes=[
            pltpu.VMEM((NR, 72, 512), F32),
            pltpu.VMEM((NR, 72, 512), F32),
            pltpu.VMEM((512, 512), BF),
            pltpu.VMEM((512, 512), BF),
            pltpu.VMEM((3, NC, 16, 256), F32),
            pltpu.VMEM((NC, 16, 256), F32),
            pltpu.VMEM((2, 5, NX, NZ, 16, 256), F32),
            pltpu.VMEM((2, 5, NX, NZ, 16, 256), F32),
            pltpu.VMEM((6, 5, 4, 16, 256), F32),
            pltpu.VMEM((6, 5, 4, 16, 256), F32),
            pltpu.VMEM((6, 5, 16, 256), F32),
            pltpu.VMEM((6, 5, 16, 256), F32),
            pltpu.VMEM((8, 128), F32),
            pltpu.VMEM((8, 128), F32),
            pltpu.VMEM((512, 512), F32),
            pltpu.VMEM((128, 256), F32),
            dma((NR,)), dma((NR,)),
            dma((3, NC)), dma((3,)),
            dma((2, NR)), dma((2,)),
            dma((NC,)), dma((NC,)),
            dma((2, 2, 6)), dma((2, 2, 6)),
            dma((2, 2, 6)), dma((2, 2, 6)),
            dma((2, 4, 2)), dma((2, 4)),
            dma((2, 5)),
        ],
        compiler_params=pltpu.CompilerParams(
            collective_id=0, has_side_effects=True, vmem_limit_bytes=48 * 1024 * 1024
        ),
        name="move",
    )(live, link, dest, lrow, coup, hcol)


def update_kernel(
    where_ref, pat_ref, aa_ref, ab_ref, ja_ref, jb_ref, l_ref, v_ref, hess_ref, o_ref,
    v_s, wj_s,
):
    t = pl.program_id(0)
    r, c = where_ref[0], where_ref[1]

    def solve(a0, a1):
        h0, l0 = split(a0)
        h1, l1 = split(a1)
        w0 = dot1(jnp.concatenate([h0, l0, h0], 1), v_s[0:256, 0:768], 1, 1)
        w1 = dot1(jnp.concatenate([h0, l0, h0, h1, l1, h1], 1), v_s[256:512, :], 1, 1)
        return w0, w1

    @pl.when(t == 0)
    def _():
        for k in (0, 1):
            hi, lo = split(v_ref[:, k * 256 : (k + 1) * 256])
            v_s[:, k * 768 : (k + 1) * 768] = jnp.concatenate([hi, hi, lo], 1)
        for u in range(5):
            j = u * NC + c
            w0, w1 = solve(
                ja_ref[u] * pat_ref[j, 0].astype(F32), jb_ref[u] * pat_ref[j, 1].astype(F32)
            )
            h0, l0 = split(w0)
            h1, l1 = split(w1)
            wj_s[u] = jnp.concatenate([h0, l0, h0, h1, l1, h1], 1)

    i = t * NR + r
    w0, w1 = solve(
        aa_ref[0, 0] * pat_ref[i, 0].astype(F32), ab_ref[0, 0] * pat_ref[i, 1].astype(F32)
    )
    h0, l0 = split(w0)
    h1, l1 = split(w1)
    wi = jnp.concatenate([h0, h0, l0, h1, h1, l1], 1)

    def put(u, value):
        for h in range(2):
            o_ref[pl.Slice(2 * u + h, 256, 10), :] = value[:, h * 128 : (h + 1) * 128]

    for u in range(5):
        j = u * NC + c
        panel = j < 2

        @pl.when((i >= j) & jnp.logical_not(panel))
        def _():
            tile = hess_ref[0, u].astype(F32)
            upd = dot1(wi, wj_s[u], 1, 1)

            @pl.when(i == j)
            def _():
                put(u, sym_block(tile) - upd)

            @pl.when(i != j)
            def _():
                put(u, tile * pat_ref[i, j].astype(F32) - upd)

        @pl.when((i < j) & jnp.logical_not(panel))
        def _():
            put(u, jnp.zeros((256, 256), F32))

        if u == 0:

            @pl.when(panel & (i >= 2))
            def _():
                put(u, jnp.where(c == 0, w0, w1))

            @pl.when(panel & (i < 2))
            def _():
                rows = pl.ds(pl.multiple_of(i * 256, 256), 256)
                lcol = jnp.where(c == 0, l_ref[rows, 0:256], l_ref[rows, 256:512])
                put(u, lcol)


def update(where, pattern, oa, ob, ja, jb, lo, v, hess):
    panel = pl.BlockSpec((1, 1, 256, 256), lambda t: (t % 2, t // 2, 0, 0))
    full = lambda *shape: pl.BlockSpec(shape, lambda t: (0,) * len(shape))
    sm = pl.BlockSpec(memory_space=pltpu.SMEM)
    return pl.pallas_call(
        update_kernel,
        grid=(10,),
        out_shape=jax.ShapeDtypeStruct((25600, 128), F32),
        in_specs=[
            sm, sm, panel, panel, full(5, 256, 256), full(5, 256, 256),
            full(512, 512), full(512, 512),
            pl.BlockSpec((1, 5, 256, 256), lambda t: (t, 0, 0, 0)),
        ],
        out_specs=pl.BlockSpec((2560, 128), lambda t: (t, 0)),
        scratch_shapes=[pltpu.VMEM((512, 1536), BF), pltpu.VMEM((5, 256, 1536), BF)],
        compiler_params=pltpu.CompilerParams(vmem_limit_bytes=48 * 1024 * 1024),
        name="update",
    )(where, pattern, oa, ob, ja, jb, lo, v, hess)


def shards(hess, coupling, dest_row, local_row, live, pattern):
    blocks = jnp.transpose(hess[:, 0, :, :, 0, :], (0, 2, 1, 3))
    where = jnp.stack([lax.axis_index("row"), lax.axis_index("col")]).astype(jnp.int32)
    oa, ob, ja, jb, lo, v = move(
        live, pattern[1, 0].reshape(1), dest_row.reshape(1, 256), local_row,
        coupling.reshape(256, 512), blocks[:, 0],
    )
    out = update(
        where, pattern, oa.reshape(2, 5, 256, 256), ob.reshape(2, 5, 256, 256),
        ja.reshape(5, 256, 256), jb.reshape(5, 256, 256), lo, v, blocks,
    )
    return out.reshape(10, 1, 256, 5, 1, 256)


def solution(mesh):
    return jax.shard_map(
        shards,
        mesh=mesh,
        in_specs=(
            P(None, "row", None, None, "col", None),
            P(("row", "col"), None, None, None),
            P(("row", "col"), None, None),
            P(("row", "col"), None),
            P(("row", "col")),
            P(),
        ),
        out_specs=P(None, "row", None, None, "col", None),
        check_vma=False,
    )
```

```python
import jax
import jax.numpy as jnp
from jax import lax
from jax.experimental import pallas as pl
from jax.experimental.pallas import tpu as pltpu
from jax.sharding import PartitionSpec as P

F32 = jnp.float32
BF = jnp.bfloat16
MESH = pl.DeviceIdType.MESH
NR, NC, NX, NZ = 8, 16, 4, 4


def dotg(a, b, ca, cb, precision=lax.Precision.HIGHEST):
    return lax.dot_general(
        a, b, (((ca,), (cb,)), ((), ())), precision=precision, preferred_element_type=F32
    )


def dot1(a, b, ca, cb):
    return lax.dot_general(a, b, (((ca,), (cb,)), ((), ())), preferred_element_type=F32)


def split(x):
    hi = x.astype(BF)
    return hi, (x - hi.astype(F32)).astype(BF)


def iota(shape, dim):
    return lax.broadcasted_iota(jnp.int32, shape, dim)


def sym_block(x):
    n = x.shape[0]
    return jnp.where(iota((n, n), 0) >= iota((n, n), 1), x, x.T)


def build_g(h00, h10, h11, link, g_ref):
    g_ref[0:256, 0:256] = sym_block(h00)
    g_ref[256:512, 256:512] = sym_block(h11)
    x = h10 * link
    g_ref[256:512, 0:256] = x
    g_ref[0:256, 256:512] = x.T
    for i in range(4):
        rows = slice(i * 128, (i + 1) * 128)
        g = g_ref[rows, :]
        on = iota((128, 512), 0) + i * 128 == iota((128, 512), 1)
        s = jnp.sum(jnp.where(on, 0.0, jnp.abs(g)), axis=1, keepdims=True) + 1.0
        g_ref[rows, :] = jnp.where(on, s, g)


def panels(s_ref, lo, hi):
    lane = iota((8, 128), 1)
    sub = iota((8, 1), 0)

    def body(b, carry):
        base = pl.multiple_of(b * 8, 8)
        rows = s_ref[pl.ds(base, 8), :]
        ra = rows[:, :128]
        cs = [
            jnp.sum(jnp.where(lane == base + j, ra, 0.0), axis=1, keepdims=True)
            for j in range(8)
        ]
        invd = jnp.zeros((8, 1), F32)
        for j in range(8):
            inv = 1.0 / cs[j][j : j + 1, :]
            m = jnp.where(sub > j, cs[j] * inv, 0.0)
            invd = jnp.where(sub == j, inv, invd)
            rows = rows - m * rows[j : j + 1, :]
            for k in range(j + 1, 8):
                cs[k] = cs[k] - m * cs[k][j : j + 1, :]
        s_ref[pl.ds(base, 8), :] = rows
        um = jnp.where(lane >= base + 8, rows[:, :128], 0.0)
        s_ref[...] = s_ref[...] - dotg(um, rows * invd, 0, 0)
        return carry

    lax.fori_loop(lo, hi, body, 0)


def diag_begin(k, g_ref, s_ref):
    o = k * 128
    s_ref[:, 0:128] = g_ref[o : o + 128, o : o + 128]
    s_ref[:, 128:256] = jnp.where(iota((128, 128), 0) == iota((128, 128), 1), 1.0, 0.0)


def diag_end(k, g_ref, s_ref, l_ref, v_ref):
    o, e = k * 128, k * 128 + 128
    r, c = iota((128, 128), 0), iota((128, 128), 1)
    u = s_ref[:, 0:128]
    s = lax.rsqrt(jnp.sum(jnp.where(r == c, u, 0.0), axis=1, keepdims=True))
    l_ref[o:e, o:e] = jnp.where(r <= c, u * s, 0.0).T
    v = s_ref[:, 128:256] * s
    v_ref[o:e, o:e] = v
    if e < 512:
        lp = dotg(g_ref[e:512, o:e], v, 1, 1)
        l_ref[e:512, o:e] = lp
        l_ref[o:e, e:512] = jnp.zeros((128, 512 - e), F32)
        v_ref[o:e, e:512] = jnp.zeros((128, 512 - e), F32)
        g_ref[e:512, e:512] = g_ref[e:512, e:512] - dotg(lp, lp, 1, 1)
    if o > 0:
        t = dotg(l_ref[o:e, 0:o], v_ref[0:o, 0:o], 1, 0)
        v_ref[o:e, 0:o] = -dotg(v, t, 1, 0)


def move_kernel(
    live_ref, link_ref, dest_ref, lrow_ref, coup_ref, hess_ref, *refs
):
    o_refs, j_refs, refs = refs[0:4], refs[4:8], refs[8:]
    (l_ref, v_ref, pack_s0, pack_s1, pack_r0, pack_r1, picks, hcol_ref, pv, pv2, pv_src), refs = (
        refs[:11],
        refs[11:],
    )
    pack_s, pack_r = (pack_s0, pack_s1), (pack_r0, pack_r1)
    p_refs, first_buf, second_buf, refs = refs[0:4], refs[4:8], refs[8:12], refs[12:]
    g_ref, s_ref = refs[:2]
    (
        a2a_s, a2a_r, p1_s, p1_r, p2_s, p2_r, p3_s, p3_r, p4_s, p4_r,
        rs_s, rs_r, ag_s, ag_r, y_s, y_r, loc, hload,
    ) = refs[2:]
    r = lax.axis_index("row")
    c = lax.axis_index("col")
    x, z = c // NZ, c % NZ
    side = r % 2
    twin = r + 1 - 2 * side
    par = c // NR

    def copy(src, dst, ss, rs, dev):
        return pltpu.make_async_remote_copy(
            src_ref=src, dst_ref=dst, send_sem=ss, recv_sem=rs, device_id=dev,
            device_id_type=MESH,
        )

    barrier = pltpu.get_barrier_semaphore()
    for d in range(1, NR):
        pl.semaphore_signal(barrier, 1, device_id=((r + d) % NR, c), device_id_type=MESH)
    for d in range(1, NC):
        pl.semaphore_signal(barrier, 1, device_id=(r, (c + d) % NC), device_id_type=MESH)
    load = pltpu.make_async_copy(hess_ref.at[:, 0], hcol_ref, hload)
    load.start()

    lane = iota((1, 256), 1)
    active = lane < live_ref[0]
    dest = dest_ref[...]
    hits = jnp.where((iota((NR, 256), 0) == dest) & active, 1.0, 0.0)
    before = jnp.where(iota((256, 256), 0) <= iota((256, 256), 1), 1.0, 0.0).astype(BF)
    cum = dot1(hits.astype(BF), before, 1, 0)
    rank = jnp.sum(hits * cum, axis=0, keepdims=True).astype(jnp.int32) - 1
    place = jnp.where(active, dest * 64 + rank, -1)
    pick = jnp.where(iota((512, 256), 0) == place, 1.0, 0.0).astype(BF)
    lr = lrow_ref[...]
    spot = jnp.where(iota((512, 256), 0) == rank + r * 64, 1.0, 0.0).astype(BF)
    lab_hi = (hits * (lr // 256).astype(F32)).astype(BF)
    lab_lo = (hits * (lr % 256).astype(F32)).astype(BF)
    labels = (
        dot1(lab_hi, spot, 1, 1) * 256.0
        + dot1(lab_lo, spot, 1, 1)
        + dot1(hits.astype(BF), spot, 1, 1)
    )
    for g in range(NR):
        pack_s[0][g, 64:72, :] = jnp.where(
            iota((8, 256), 0) == 0, labels[g : g + 1, 0:256], labels[g : g + 1, 256:512]
        )

    def pack(k):
        rows = jnp.concatenate(
            [coup_ref[pl.Slice(2 * h + k, 256, 4), :] for h in range(2)], axis=1
        )
        c_hi, c_lo = split(rows)
        packed = dot1(pick, c_hi, 1, 0) + dot1(pick, c_lo, 1, 0)
        pack_s[k][:, 0:64, :] = packed.reshape(NR, 64, 256)

    def a2a(k, d):
        to = (r + d) % NR
        return copy(
            pack_s[k].at[to], pack_r[k].at[r], a2a_s.at[k, d], a2a_r.at[k, d], (to, c)
        )

    far_first = (4, 3, 5, 2, 6, 1, 7)
    pack(0)
    pl.semaphore_wait(barrier, NR - 1 + NC - 1)
    for d in far_first:
        a2a(0, d).start()
    pack_r[0][r] = pack_s[0][r]
    pack(1)
    for d in far_first:
        a2a(1, d).start()
    pack_r[1][r] = pack_s[1][r]

    sources = ((0, 0), (1, 0), (1, 1))

    def p1(b, d):
        to = (sources[b][1] + d) % NC
        return copy(pv_src.at[to], pv.at[b, to], p1_s.at[b, d], p1_r.at[b], (sources[b][0], to))

    load.wait()
    pv_src[...] = hcol_ref[0].astype(F32).reshape(NC, 16, 256)
    for b, (sr, sc) in enumerate(sources):

        @pl.when((r == sr) & (c == sc))
        def _():
            for d in range(1, NC):
                p1(b, d).start()
            pv[b, sc] = pv_src[sc]

    def p2(k, d):
        blocks = pl.ds(0, 1) if k == 0 else pl.ds(1, 2)
        to = (k + d) % NR
        part = pv.at[blocks, c]
        return copy(part, part, p2_s.at[k, d], p2_r.at[k], (to, c))

    def p2_start():
        for b, (sr, sc) in enumerate(sources):

            @pl.when((r == sr) & (c != sc))
            def _():
                p1(b, 1).wait_recv()

        for k in (0, 1):

            @pl.when(r == k)
            def _():
                for d in range(1, NR):
                    p2(k, d).start()

    eight = pl.ds(pl.multiple_of(8 * side, 8), 8)

    def p3(d):
        return copy(
            pv.at[:, c, eight], pv2.at[:, c, eight], p3_s.at[d], p3_r.at[d], (r, (c + d) % NC)
        )

    def p3_start():
        for k in (0, 1):

            @pl.when(r != k)
            def _():
                p2(k, 1).wait_recv()

        for d in range(1, NC):
            p3(d).start()
        pv2[:, c, eight] = pv[:, c, eight]

    def p4():
        part = pv2.at[:, :, eight]
        return copy(part, part, p4_s, p4_r, (twin, c))

    def p4_start():
        for d in range(1, NC):
            p3(d).wait_recv()
        p4().start()

    def labels_in():
        lab = jnp.zeros((8, 256), F32)
        for g in range(NR):
            lab = lab + pack_r[0][g, 64:72, :]
        return jnp.concatenate([lab[0:1], lab[1:2]], axis=1).astype(jnp.int32) - 1

    def picks_in(lab, p):
        for t2 in range(5):
            t = 2 * t2 + p
            pick = jnp.where(iota((256, 512), 0) + t * 256 == lab, 1.0, 0.0).astype(BF)
            picks[p, t2 * 256 : t2 * 256 + 256, :] = pick

    def fill(k, p):
        rows = jnp.concatenate([pack_r[k][g, 0:64, :] for g in range(NR)], axis=0)
        hi, lo = split(rows)
        mine = jnp.where(c == k, 1.0, 0.0)
        got = dot1(picks[p], hi, 1, 0) + dot1(picks[p], lo, 1, 0)
        for t2 in range(5):
            part = got[t2 * 256 : t2 * 256 + 256] + hcol_ref[2 * t2 + p].astype(F32) * mine
            for h in range(2):
                p_refs[2 * k + h][p, t2] = part[:, h * 128 : (h + 1) * 128].reshape(
                    NX, NZ, 16, 128
                )

    def along_x(n):
        return (r, (n % NX) * NZ + z)

    def along_z(n):
        return (r, x * NZ + n % NZ)

    def unit(ref, g, big, n, p):
        n = n % 4
        if g % 2 == 0:
            return ref.at[p, :, n] if big else ref.at[p, :, x, n]
        return ref.at[p, :, :, n] if big else ref.at[p, :, n, z]

    def ring(g, big):
        return (x, along_x) if (g % 2 == 0) == big else (z, along_z)

    def rs(g, phase, m):
        n, dev = ring(g, phase == 0)
        buf = (first_buf, second_buf)[phase][g]
        at, p, to = (
            (n + 2, 0, n + 1), (n + 1, 1, n + 1), (n + 1, 0, n + 1),
            (n + 2, 1, n + 3), (n + 3, 0, n + 3), (n + 3, 1, n + 3),
        )[m]
        return copy(
            unit(p_refs[g], g, phase == 0, at, p), buf.at[m],
            rs_s.at[g, phase, m], rs_r.at[g, phase, m], dev(to),
        )

    def rs_start(k, phase, p):
        for m in ((0, 4), (3, 1))[p]:
            for g in (2 * k, 2 * k + 1):
                rs(g, phase, m).start()

    def rs_middle(k, phase):
        for m_in, m_out, step, p in ((0, 2, 1, 0), (3, 5, 3, 1)):
            for g in (2 * k, 2 * k + 1):
                n, dev = ring(g, phase == 0)
                rs(g, phase, m_in).wait_recv()
                ref = unit(p_refs[g], g, phase == 0, n + step, p)
                ref[...] = ref[...] + (first_buf, second_buf)[phase][g][m_in]
                rs(g, phase, m_out).start()

    def rs_end(k, phase):
        for p, (m1, m2) in enumerate(((4, 2), (1, 5))):
            for g in (2 * k, 2 * k + 1):
                n, dev = ring(g, phase == 0)
                buf = (first_buf, second_buf)[phase][g]
                rs(g, phase, m1).wait_recv()
                rs(g, phase, m2).wait_recv()
                ref = unit(p_refs[g], g, phase == 0, n, p)
                ref[...] = ref[...] + (buf[m1] + buf[m2])
            if phase == 0:
                rs_start(k, 1, p)

    def ag(g, phase, m):
        n, dev = ring(g, phase == 1)
        want = (lambda i: 0) if phase == 0 else (lambda i: i % 4 // 2) if g % 2 == 0 else (lambda i: par)
        back = want(n) if phase == 1 and g % 2 == 0 else 1 - want(n)
        at, p, to = (
            (n, want(n + 1), n + 1), (n, 1 - want(n + 1), n + 1), (n, want(n + 3), n + 3),
            (n, 1 - want(n + 3), n + 3), (n + 3, want(n), n + 1), (n + 1, back, n + 3),
        )[m]
        src = unit(o_refs[g], g, phase == 1, at, p)
        return copy(src, src, ag_s.at[g, phase, m], ag_r.at[g, phase, m], dev(to))

    def ag_own(k):
        keeps = [
            pltpu.make_async_copy(
                p_refs[g].at[:, :, x, z], o_refs[g].at[:, :, x, z], loc.at[g, 4]
            )
            for g in (2 * k, 2 * k + 1)
        ]
        for keep in keeps:
            keep.start()
        for keep in keeps:
            keep.wait()

    def ag_start(k):
        for m in (0, 3, 1, 2):
            for g in (2 * k, 2 * k + 1):
                ag(g, 0, m).start()

    def ag_forward(k):
        for m_in, m_out in ((0, 4), (3, 5)):
            for g in (2 * k, 2 * k + 1):
                ag(g, 0, m_in).wait_recv()
                ag(g, 0, m_out).start()

    def big_start(k):
        for m in (1, 2, 4, 5):
            for g in (2 * k, 2 * k + 1):
                ag(g, 0, m).wait_recv()
        for m in (0, 2):
            for g in (2 * k, 2 * k + 1):
                ag(g, 1, m).start()
        y_source(k, 0)

    def big_forward(k):
        for g in (2 * k, 2 * k + 1):
            ag(g, 1, 0).wait_recv()
            ag(g, 1, 4).start()
        for g in (2 * k, 2 * k + 1):
            ag(g, 1, 2).wait_recv()
            if g % 2 == 0:
                ag(g, 1, 5).start()
            ag(g, 1, 3).start()
            ag(g, 1, 1).start()
        y_source(k, 1)
        y_source(k, 2)

    def big_last(k):
        ag(2 * k, 1, 4).wait_recv()
        ag(2 * k, 1, 5).wait_recv()
        ag(2 * k + 1, 1, 4).wait_recv()
        y_source(k, 3)
        ag(2 * k + 1, 1, 3).wait_recv()
        ag(2 * k + 1, 1, 5).start()

    def big_end(k):
        ag(2 * k, 1, 1).wait_recv()
        ag(2 * k, 1, 3).wait_recv()
        ag(2 * k + 1, 1, 1).wait_recv()
        ag(2 * k + 1, 1, 5).wait_recv()

    y, ys = r // 2, (c % NR) // 2
    chain = side == c % 2
    hop = ((y - ys + 4) % 4, (ys - y + 4) % 4)

    def piece(g, i):
        return ring(g, True)[0] + (0, 3, 1, 2)[i]

    def y_refs(g, i):
        n = piece(g, i) % 4
        if g % 2 == 0:
            return o_refs[g].at[par, :, n], j_refs[g].at[:, n]
        return o_refs[g].at[par, :, :, n], j_refs[g].at[:, :, n]

    def y_copy(g, i, to_twin, from_o):
        o, j = y_refs(g, i)
        step = 2 if g % 2 == 0 else 6
        to = twin if to_twin else (r + step) % NR
        return copy(
            o if from_o else j, j, y_s.at[g, i, to_twin], y_r.at[g, i], (to, c)
        )

    def y_local(g, i):
        o, j = y_refs(g, i)
        return pltpu.make_async_copy(o, j, loc.at[g, i])

    def y_source(k, i):
        for g in (2 * k, 2 * k + 1):

            @pl.when(chain & (hop[g % 2] == 0))
            def _():
                y_copy(g, i, 0, True).start()
                y_copy(g, i, 1, True).start()
                y_local(g, i).start()

    def y_step(k, step):
        for far in (1, 2, 3):
            for g in (2 * k, 2 * k + 1):
                i = step - far
                if 0 <= i < 4:

                    @pl.when(chain & (hop[g % 2] == far))
                    def _():
                        y_copy(g, i, 0, False).wait_recv()
                        if far < 3:
                            y_copy(g, i, 0, False).start()
                        y_copy(g, i, 1, False).start()

    def y_last(k):
        for g in (2 * k, 2 * k + 1):
            for i in range(4):

                @pl.when(jnp.logical_not(chain))
                def _():
                    y_copy(g, i, 0, False).wait_recv()

                @pl.when(chain & (hop[g % 2] == 0))
                def _():
                    y_local(g, i).wait()

                @pl.when(chain & (hop[g % 2] < 3))
                def _():
                    y_copy(g, i, 0, False).wait_send()

                @pl.when(chain)
                def _():
                    y_copy(g, i, 1, False).wait_send()

    done = []

    def f(count):
        for _ in range(count):
            q = len(done)
            done.append(q)
            k, part = q // 8, q % 8
            if q == 0:
                p4().wait_recv()
                build_g(
                    pv2[0].reshape(256, 256), pv2[1].reshape(256, 256),
                    pv2[2].reshape(256, 256), link_ref[0].astype(F32), g_ref,
                )
            if part == 0:
                diag_begin(k, g_ref, s_ref)
            panels(s_ref, part * 2, part * 2 + 2)
            if part == 7:
                diag_end(k, g_ref, s_ref, l_ref, v_ref)

    def e0(k):
        for d in range(1, NR):
            a2a(k, d).wait_recv()
        if k == 0:
            lab = labels_in()
        for p in (0, 1):
            if k == 0:
                picks_in(lab, p)
            fill(k, p)
            rs_start(k, 0, p)

    p2_start()
    e0(0)
    p3_start()
    e0(1)
    rs_middle(0, 0)
    p4_start()
    f(2)
    rs_end(0, 0)
    rs_middle(1, 0)
    f(1)
    rs_middle(0, 1)
    f(1)
    rs_end(0, 1)
    ag_own(0)
    ag_start(0)
    f(2)
    ag_forward(0)
    rs_end(1, 0)
    f(1)
    big_start(0)
    rs_middle(1, 1)
    f(2)
    rs_end(1, 1)
    ag_own(1)
    ag_start(1)
    big_forward(0)
    f(1)
    y_step(0, 1)
    ag_forward(1)
    f(1)
    big_start(1)
    y_step(0, 2)
    f(1)
    big_last(0)
    y_step(0, 3)
    big_forward(1)
    y_step(1, 1)
    y_step(0, 4)
    f(2)
    y_step(0, 5)
    y_step(1, 2)
    f(1)
    big_last(1)
    f(3)
    y_step(0, 6)
    big_end(0)
    y_step(1, 3)
    f(4)
    y_step(1, 4)
    f(4)
    y_step(1, 5)
    f(4)
    y_step(1, 6)
    f(2)
    big_end(1)
    for k in (0, 1):
        y_last(k)

    for g in range(4):
        for phase in (0, 1):
            for m in range(6):
                rs(g, phase, m).wait_send()
                ag(g, phase, m).wait_send()
    for k in (0, 1):
        for d in range(1, NR):
            a2a(k, d).wait_send()
    for b, (sr, sc) in enumerate(sources):

        @pl.when((r == sr) & (c == sc))
        def _():
            for d in range(1, NC):
                p1(b, d).wait_send()

    for k in (0, 1):

        @pl.when(r == k)
        def _():
            for d in range(1, NR):
                p2(k, d).wait_send()

    for d in range(1, NC):
        p3(d).wait_send()
    p4().wait_send()


def move(live, link, dest, lrow, coup, blocks):
    vm = pl.BlockSpec(memory_space=pltpu.VMEM)
    sm = pl.BlockSpec(memory_space=pltpu.SMEM)
    hb = pl.BlockSpec(memory_space=pltpu.HBM)
    dma = pltpu.SemaphoreType.DMA
    group = jax.ShapeDtypeStruct((2, 5, NX, NZ, 16, 128), F32)
    cols = jax.ShapeDtypeStruct((5, NX, NZ, 16, 128), F32)
    square = jax.ShapeDtypeStruct((512, 512), F32)
    return pl.pallas_call(
        move_kernel,
        out_shape=(group,) * 4 + (cols,) * 4 + (square, square),
        in_specs=[sm, sm, vm, vm, vm, hb],
        out_specs=[vm] * 10,
        scratch_shapes=[
            pltpu.VMEM((NR, 72, 256), F32),
            pltpu.VMEM((NR, 64, 256), F32),
            pltpu.VMEM((NR, 72, 256), F32),
            pltpu.VMEM((NR, 64, 256), F32),
            pltpu.VMEM((2, 1280, 512), BF),
            pltpu.VMEM((10, 256, 256), BF),
            pltpu.VMEM((3, NC, 16, 256), F32),
            pltpu.VMEM((3, NC, 16, 256), F32),
            pltpu.VMEM((NC, 16, 256), F32),
        ]
        + [pltpu.VMEM((2, 5, NX, NZ, 16, 128), F32)] * 4
        + [pltpu.VMEM((6, 5, 4, 16, 128), F32)] * 4
        + [pltpu.VMEM((6, 5, 16, 128), F32)] * 4
        + [
            pltpu.VMEM((512, 512), F32),
            pltpu.VMEM((128, 256), F32),
            dma((2, NR)), dma((2, NR)),
            dma((3, NC)), dma((3,)),
            dma((2, NR)), dma((2,)),
            dma((NC,)), dma((NC,)),
            dma(()), dma(()),
            dma((4, 2, 6)), dma((4, 2, 6)),
            dma((4, 2, 6)), dma((4, 2, 6)),
            dma((4, 4, 2)), dma((4, 4)),
            dma((4, 5)), dma(()),
        ],
        compiler_params=pltpu.CompilerParams(
            collective_id=0, has_side_effects=True, vmem_limit_bytes=40 * 1024 * 1024
        ),
        name="move",
    )(live, link, dest, lrow, coup, blocks)


def update_kernel(
    where_ref, pat_ref, a0_ref, a1_ref, a2_ref, a3_ref, j0_ref, j1_ref, j2_ref, j3_ref,
    l_ref, v_ref, hess_ref, o_ref, v_s, wj_s,
):
    s = pl.program_id(0)
    r, c = where_ref[0], where_ref[1]

    def wide(left, right):
        return jnp.concatenate([left, right], axis=1)

    def solve(a0, a1):
        h0, l0 = split(a0)
        h1, l1 = split(a1)
        w0 = dot1(jnp.concatenate([h0, l0, h0], 1), v_s[0:256, 0:768], 1, 1)
        w1 = dot1(jnp.concatenate([h0, l0, h0, h1, l1, h1], 1), v_s[256:512, :], 1, 1)
        return w0, w1

    @pl.when(s == 0)
    def _():
        for k in (0, 1):
            hi, lo = split(v_ref[:, k * 256 : (k + 1) * 256])
            v_s[:, k * 768 : (k + 1) * 768] = jnp.concatenate([hi, hi, lo], 1)

        def column(u, carry):
            j = u * NC + c
            w0, w1 = solve(
                wide(j0_ref[u], j1_ref[u]) * pat_ref[j, 0].astype(F32),
                wide(j2_ref[u], j3_ref[u]) * pat_ref[j, 1].astype(F32),
            )
            h0, l0 = split(w0)
            h1, l1 = split(w1)
            wj_s[u] = jnp.concatenate([h0, l0, h0, h1, l1, h1], 1)
            return carry

        lax.fori_loop(0, 5, column, 0)

    rows = (s * 2 * NR + r, s * 2 * NR + NR + r)

    def links(k):
        return jnp.where(
            iota((512, 1), 0) < 256, pat_ref[rows[0], k], pat_ref[rows[1], k]
        ).astype(F32)

    def pair(left, right):
        return wide(left[:, s].reshape(512, 128), right[:, s].reshape(512, 128))

    w0, w1 = solve(pair(a0_ref, a1_ref) * links(0), pair(a2_ref, a3_ref) * links(1))
    h0, l0 = split(w0)
    h1, l1 = split(w1)
    wi = jnp.concatenate([h0, h0, l0, h1, h1, l1], 1)

    def put(p, u, value):
        for h in range(2):
            o_ref[pl.Slice(2560 * p + 2 * u + h, 256, 10), :] = value[:, h * 128 : (h + 1) * 128]

    for u in range(5):
        j = u * NC + c
        panel = j < 2

        @pl.when((u < s) & jnp.logical_not(panel))
        def _():
            upd = dot1(wi, wj_s[u], 1, 1)
            for p in (0, 1):
                tile = hess_ref[2 * s + p, u].astype(F32)
                put(p, u, tile * pat_ref[rows[p], j].astype(F32) - upd[p * 256 : p * 256 + 256])

        for p in (0, 1):
            i = rows[p]

            @pl.when((u == s) & (i >= j) & jnp.logical_not(panel))
            def _():
                tile = hess_ref[2 * s + p, u].astype(F32)
                upd = dot1(wi[p * 256 : p * 256 + 256], wj_s[u], 1, 1)

                @pl.when(i == j)
                def _():
                    put(p, u, sym_block(tile) - upd)

                @pl.when(i != j)
                def _():
                    put(p, u, tile * pat_ref[i, j].astype(F32) - upd)

            @pl.when((i < j) & jnp.logical_not(panel))
            def _():
                put(p, u, jnp.zeros((256, 256), F32))

            if u == 0:

                @pl.when(panel & (i >= 2))
                def _():
                    put(p, u, jnp.where(c == 0, w0, w1)[p * 256 : p * 256 + 256])

                if p == 0:

                    @pl.when(panel & (i < 2))
                    def _():
                        at = pl.ds(pl.multiple_of(i * 256, 256), 256)
                        put(p, u, jnp.where(c == 0, l_ref[at, 0:256], l_ref[at, 256:512]))


def update(where, pattern, moved, hess):
    vm = pl.BlockSpec(memory_space=pltpu.VMEM)
    sm = pl.BlockSpec(memory_space=pltpu.SMEM)
    return pl.pallas_call(
        update_kernel,
        grid=(5,),
        out_shape=jax.ShapeDtypeStruct((25600, 128), F32),
        in_specs=[sm, sm] + [vm] * 11,
        out_specs=pl.BlockSpec((5120, 128), lambda s: (s, 0)),
        scratch_shapes=[pltpu.VMEM((512, 1536), BF), pltpu.VMEM((5, 256, 1536), BF)],
        compiler_params=pltpu.CompilerParams(vmem_limit_bytes=20 * 1024 * 1024),
        name="update",
    )(
        where, pattern, *[o.reshape(2, 5, 256, 128) for o in moved[0:4]],
        *[j.reshape(5, 256, 128) for j in moved[4:8]], *moved[8:], hess,
    )


def shards(hess, coupling, dest_row, local_row, live, pattern):
    blocks = jnp.transpose(hess[:, 0, :, :, 0, :], (0, 2, 1, 3))
    where = jnp.stack([lax.axis_index("row"), lax.axis_index("col")]).astype(jnp.int32)
    coup = jnp.transpose(coupling.reshape(256, 2, 2, 128), (0, 2, 1, 3)).reshape(1024, 128)
    moved = move(
        live, pattern[1, 0].reshape(1), dest_row.reshape(1, 256), local_row, coup, blocks
    )
    out = update(where, pattern, moved, blocks)
    return out.reshape(10, 1, 256, 5, 1, 256)


def solution(mesh):
    return jax.shard_map(
        shards,
        mesh=mesh,
        in_specs=(
            P(None, "row", None, None, "col", None),
            P(("row", "col"), None, None, None),
            P(("row", "col"), None, None),
            P(("row", "col"), None),
            P(("row", "col")),
            P(),
        ),
        out_specs=P(None, "row", None, None, "col", None),
        check_vma=False,
    )
```

```python
import jax
import jax.numpy as jnp
from jax import lax
from jax.experimental import pallas as pl
from jax.experimental.pallas import tpu as pltpu
from jax.sharding import PartitionSpec as P

F32 = jnp.float32
BF = jnp.bfloat16
MESH = pl.DeviceIdType.MESH
NR, NC, NX, NZ = 8, 16, 4, 4


def dotg(a, b, ca, cb, precision=lax.Precision.HIGHEST):
    return lax.dot_general(
        a, b, (((ca,), (cb,)), ((), ())), precision=precision, preferred_element_type=F32
    )


def dot1(a, b, ca, cb):
    return lax.dot_general(a, b, (((ca,), (cb,)), ((), ())), preferred_element_type=F32)


def split(x):
    hi = x.astype(BF)
    return hi, (x - hi.astype(F32)).astype(BF)


def iota(shape, dim):
    return lax.broadcasted_iota(jnp.int32, shape, dim)


def sym_block(x):
    n = x.shape[0]
    return jnp.where(iota((n, n), 0) >= iota((n, n), 1), x, x.T)


def build_g(h00, h10, h11, link, g_ref):
    g_ref[0:256, 0:256] = sym_block(h00)
    g_ref[256:512, 256:512] = sym_block(h11)
    x = h10 * link
    g_ref[256:512, 0:256] = x
    g_ref[0:256, 256:512] = x.T
    for i in range(4):
        rows = slice(i * 128, (i + 1) * 128)
        g = g_ref[rows, :]
        on = iota((128, 512), 0) + i * 128 == iota((128, 512), 1)
        s = jnp.sum(jnp.where(on, 0.0, jnp.abs(g)), axis=1, keepdims=True) + 1.0
        g_ref[rows, :] = jnp.where(on, s, g)


def panels(s_ref, lo, hi):
    lane = iota((8, 128), 1)
    sub = iota((8, 1), 0)

    def body(b, carry):
        base = pl.multiple_of(b * 8, 8)
        rows = s_ref[pl.ds(base, 8), :]
        ra = rows[:, :128]
        cs = [
            jnp.sum(jnp.where(lane == base + j, ra, 0.0), axis=1, keepdims=True)
            for j in range(8)
        ]
        invd = jnp.zeros((8, 1), F32)
        for j in range(8):
            inv = 1.0 / cs[j][j : j + 1, :]
            m = jnp.where(sub > j, cs[j] * inv, 0.0)
            invd = jnp.where(sub == j, inv, invd)
            rows = rows - m * rows[j : j + 1, :]
            for k in range(j + 1, 8):
                cs[k] = cs[k] - m * cs[k][j : j + 1, :]
        s_ref[pl.ds(base, 8), :] = rows
        um = jnp.where(lane >= base + 8, rows[:, :128], 0.0)
        s_ref[...] = s_ref[...] - dotg(um, rows * invd, 0, 0)
        return carry

    lax.fori_loop(lo, hi, body, 0)


def diag_begin(k, g_ref, s_ref):
    o = k * 128
    s_ref[:, 0:128] = g_ref[o : o + 128, o : o + 128]
    s_ref[:, 128:256] = jnp.where(iota((128, 128), 0) == iota((128, 128), 1), 1.0, 0.0)


def diag_end(k, g_ref, s_ref, l_ref, v_ref):
    o, e = k * 128, k * 128 + 128
    r, c = iota((128, 128), 0), iota((128, 128), 1)
    u = s_ref[:, 0:128]
    s = lax.rsqrt(jnp.sum(jnp.where(r == c, u, 0.0), axis=1, keepdims=True))
    l_ref[o:e, o:e] = jnp.where(r <= c, u * s, 0.0).T
    v = s_ref[:, 128:256] * s
    v_ref[o:e, o:e] = v
    if e < 512:
        lp = dotg(g_ref[e:512, o:e], v, 1, 1)
        l_ref[e:512, o:e] = lp
        l_ref[o:e, e:512] = jnp.zeros((128, 512 - e), F32)
        v_ref[o:e, e:512] = jnp.zeros((128, 512 - e), F32)
        g_ref[e:512, e:512] = g_ref[e:512, e:512] - dotg(lp, lp, 1, 1)
    if o > 0:
        t = dotg(l_ref[o:e, 0:o], v_ref[0:o, 0:o], 1, 0)
        v_ref[o:e, 0:o] = -dotg(v, t, 1, 0)


def move_kernel(
    live_ref, pat_hbm, dest_hbm, lrow_hbm, coup_hbm, hess_ref, *refs
):
    o_refs, j_refs, refs = refs[0:4], refs[4:8], refs[8:]
    (l_ref, v_ref, pack_s0, pack_s1, pack_r0, pack_r1, picks, hcol_ref, pv, pv2, pv_src), refs = (
        refs[:11],
        refs[11:],
    )
    pack_s, pack_r = (pack_s0, pack_s1), (pack_r0, pack_r1)
    p_refs, first_buf, second_buf, refs = refs[0:4], refs[4:8], refs[8:12], refs[12:]
    g_ref, s_ref, pat_ref, dest_ref, lrow_ref, coup_ref, lead_ref = refs[:7]
    (
        a2a_s, a2a_r, p1_s, p1_r, p2_s, p2_r, p3_s, p3_r, p4_s, p4_r,
        rs_s, rs_r, ag_s, ag_r, y_s, y_r, loc, hload,
    ) = refs[7:]
    r = lax.axis_index("row")
    c = lax.axis_index("col")
    x, z = c // NZ, c % NZ
    side = r % 2
    twin = r + 1 - 2 * side
    par = c // NR

    def copy(src, dst, ss, rs, dev):
        return pltpu.make_async_remote_copy(
            src_ref=src, dst_ref=dst, send_sem=ss, recv_sem=rs, device_id=dev,
            device_id_type=MESH,
        )

    barrier = pltpu.get_barrier_semaphore()
    for d in range(1, NR):
        pl.semaphore_signal(barrier, 1, device_id=((r + d) % NR, c), device_id_type=MESH)
    for d in range(1, NC):
        pl.semaphore_signal(barrier, 1, device_id=(r, (c + d) % NC), device_id_type=MESH)
    loads = [
        pltpu.make_async_copy(src, dst, hload.at[i])
        for i, (src, dst) in enumerate(
            (
                (dest_hbm, dest_ref),
                (lrow_hbm, lrow_ref),
                (coup_hbm, coup_ref),
                (hess_ref.at[0, 0], lead_ref),
                (pat_hbm, pat_ref),
                (hess_ref.at[:, 0], hcol_ref),
            )
        )
    ]
    for load in loads:
        load.start()
    for load in loads[:4]:
        load.wait()

    lane = iota((1, 256), 1)
    active = lane < live_ref[0]
    dest = dest_ref[...]
    hits = jnp.where((iota((NR, 256), 0) == dest) & active, 1.0, 0.0)
    before = jnp.where(iota((256, 256), 0) <= iota((256, 256), 1), 1.0, 0.0).astype(BF)
    cum = dot1(hits.astype(BF), before, 1, 0)
    rank = jnp.sum(hits * cum, axis=0, keepdims=True).astype(jnp.int32) - 1
    place = jnp.where(active, dest * 64 + rank, -1)
    pick = jnp.where(iota((512, 256), 0) == place, 1.0, 0.0).astype(BF)
    lr = lrow_ref[...]
    spot = jnp.where(iota((512, 256), 0) == rank + r * 64, 1.0, 0.0).astype(BF)
    lab_hi = (hits * (lr // 256).astype(F32)).astype(BF)
    lab_lo = (hits * (lr % 256).astype(F32)).astype(BF)
    labels = (
        dot1(lab_hi, spot, 1, 1) * 256.0
        + dot1(lab_lo, spot, 1, 1)
        + dot1(hits.astype(BF), spot, 1, 1)
    )
    for g in range(NR):
        pack_s[0][g, 64:72, :] = jnp.where(
            iota((8, 256), 0) == 0, labels[g : g + 1, 0:256], labels[g : g + 1, 256:512]
        )

    def pack(k):
        rows = jnp.concatenate(
            [coup_ref[pl.Slice(2 * h + k, 256, 4), :] for h in range(2)], axis=1
        )
        c_hi, c_lo = split(rows)
        packed = dot1(pick, c_hi, 1, 0) + dot1(pick, c_lo, 1, 0)
        pack_s[k][:, 0:64, :] = packed.reshape(NR, 64, 256)

    def a2a(k, d):
        to = (r + d) % NR
        return copy(
            pack_s[k].at[to], pack_r[k].at[r], a2a_s.at[k, d], a2a_r.at[k, d], (to, c)
        )

    far_first = (4, 3, 5, 2, 6, 1, 7)
    pv_src[...] = lead_ref[...].astype(F32).reshape(NC, 16, 256)
    pack(0)
    pl.semaphore_wait(barrier, NR - 1 + NC - 1)

    sources = ((0, 0), (1, 0), (1, 1))

    def p1(b, d):
        to = (sources[b][1] + d) % NC
        return copy(pv_src.at[to], pv.at[b, to], p1_s.at[b, d], p1_r.at[b], (sources[b][0], to))

    for b, (sr, sc) in enumerate(sources):

        @pl.when((r == sr) & (c == sc))
        def _():
            for d in range(1, NC):
                p1(b, d).start()
            pv[b, sc] = pv_src[sc]

    for d in far_first:
        a2a(0, d).start()
    pack_r[0][r] = pack_s[0][r]
    pack(1)

    def p2(k, d):
        blocks = pl.ds(0, 1) if k == 0 else pl.ds(1, 2)
        to = (k + d) % NR
        part = pv.at[blocks, c]
        return copy(part, part, p2_s.at[k, d], p2_r.at[k], (to, c))

    def p2_start():
        for b, (sr, sc) in enumerate(sources):

            @pl.when((r == sr) & (c != sc))
            def _():
                p1(b, 1).wait_recv()

        for k in (0, 1):

            @pl.when(r == k)
            def _():
                for d in range(1, NR):
                    p2(k, d).start()

    eight = pl.ds(pl.multiple_of(8 * side, 8), 8)

    def p3(d):
        return copy(
            pv.at[:, c, eight], pv2.at[:, c, eight], p3_s.at[d], p3_r.at[d], (r, (c + d) % NC)
        )

    def p3_start():
        for k in (0, 1):

            @pl.when(r != k)
            def _():
                p2(k, 1).wait_recv()

        for d in range(1, NC):
            p3(d).start()
        pv2[:, c, eight] = pv[:, c, eight]

    def p4():
        part = pv2.at[:, :, eight]
        return copy(part, part, p4_s, p4_r, (twin, c))

    def p4_start():
        for d in range(1, NC):
            p3(d).wait_recv()
        p4().start()

    p2_start()
    for d in far_first:
        a2a(1, d).start()
    pack_r[1][r] = pack_s[1][r]
    p3_start()
    loads[4].wait()
    loads[5].wait()

    def labels_in():
        lab = jnp.zeros((8, 256), F32)
        for g in range(NR):
            lab = lab + pack_r[0][g, 64:72, :]
        return jnp.concatenate([lab[0:1], lab[1:2]], axis=1).astype(jnp.int32) - 1

    def picks_in(lab, p):
        for t2 in range(5):
            t = 2 * t2 + p
            pick = jnp.where(iota((256, 512), 0) + t * 256 == lab, 1.0, 0.0).astype(BF)
            picks[p, t2 * 256 : t2 * 256 + 256, :] = pick

    def fill(k, p):
        rows = jnp.concatenate([pack_r[k][g, 0:64, :] for g in range(NR)], axis=0)
        hi, lo = split(rows)
        mine = jnp.where(c == k, 1.0, 0.0)
        got = dot1(picks[p], hi, 1, 0) + dot1(picks[p], lo, 1, 0)
        for t2 in range(5):
            part = got[t2 * 256 : t2 * 256 + 256] + hcol_ref[2 * t2 + p].astype(F32) * mine
            for h in range(2):
                p_refs[2 * k + h][p, t2] = part[:, h * 128 : (h + 1) * 128].reshape(
                    NX, NZ, 16, 128
                )

    def along_x(n):
        return (r, (n % NX) * NZ + z)

    def along_z(n):
        return (r, x * NZ + n % NZ)

    def unit(ref, g, big, n, p):
        n = n % 4
        if g % 2 == 0:
            return ref.at[p, :, n] if big else ref.at[p, :, x, n]
        return ref.at[p, :, :, n] if big else ref.at[p, :, n, z]

    def ring(g, big):
        return (x, along_x) if (g % 2 == 0) == big else (z, along_z)

    def rs(g, phase, m):
        n, dev = ring(g, phase == 0)
        buf = (first_buf, second_buf)[phase][g]
        at, p, to = (
            (n + 2, 0, n + 1), (n + 1, 1, n + 1), (n + 1, 0, n + 1),
            (n + 2, 1, n + 3), (n + 3, 0, n + 3), (n + 3, 1, n + 3),
        )[m]
        return copy(
            unit(p_refs[g], g, phase == 0, at, p), buf.at[m],
            rs_s.at[g, phase, m], rs_r.at[g, phase, m], dev(to),
        )

    def rs_start(k, phase, p):
        for m in ((0, 4), (3, 1))[p]:
            for g in (2 * k, 2 * k + 1):
                rs(g, phase, m).start()

    def rs_middle(k, phase):
        for m_in, m_out, step, p in ((0, 2, 1, 0), (3, 5, 3, 1)):
            for g in (2 * k, 2 * k + 1):
                n, dev = ring(g, phase == 0)
                rs(g, phase, m_in).wait_recv()
                ref = unit(p_refs[g], g, phase == 0, n + step, p)
                ref[...] = ref[...] + (first_buf, second_buf)[phase][g][m_in]
                rs(g, phase, m_out).start()

    def rs_end(k, phase):
        for p, (m1, m2) in enumerate(((4, 2), (1, 5))):
            for g in (2 * k, 2 * k + 1):
                n, dev = ring(g, phase == 0)
                buf = (first_buf, second_buf)[phase][g]
                rs(g, phase, m1).wait_recv()
                rs(g, phase, m2).wait_recv()
                ref = unit(p_refs[g], g, phase == 0, n, p)
                ref[...] = ref[...] + (buf[m1] + buf[m2])
            if phase == 0:
                rs_start(k, 1, p)

    def ag(g, phase, m):
        n, dev = ring(g, phase == 1)
        want = (lambda i: 0) if phase == 0 else (lambda i: i % 4 // 2) if g % 2 == 0 else (lambda i: par)
        back = want(n) if phase == 1 and g % 2 == 0 else 1 - want(n)
        at, p, to = (
            (n, want(n + 1), n + 1), (n, 1 - want(n + 1), n + 1), (n, want(n + 3), n + 3),
            (n, 1 - want(n + 3), n + 3), (n + 3, want(n), n + 1), (n + 1, back, n + 3),
        )[m]
        src = unit(o_refs[g], g, phase == 1, at, p)
        return copy(src, src, ag_s.at[g, phase, m], ag_r.at[g, phase, m], dev(to))

    def ag_own(k):
        keeps = [
            pltpu.make_async_copy(
                p_refs[g].at[:, :, x, z], o_refs[g].at[:, :, x, z], loc.at[g, 4]
            )
            for g in (2 * k, 2 * k + 1)
        ]
        for keep in keeps:
            keep.start()
        for keep in keeps:
            keep.wait()

    def ag_start(k):
        for m in (0, 3, 1, 2):
            for g in (2 * k, 2 * k + 1):
                ag(g, 0, m).start()

    def ag_forward(k):
        for m_in, m_out in ((0, 4), (3, 5)):
            for g in (2 * k, 2 * k + 1):
                ag(g, 0, m_in).wait_recv()
                ag(g, 0, m_out).start()

    def big_start(k):
        for m in (1, 2, 4, 5):
            for g in (2 * k, 2 * k + 1):
                ag(g, 0, m).wait_recv()
        for m in (0, 2):
            for g in (2 * k, 2 * k + 1):
                ag(g, 1, m).start()
        y_source(k, 0)

    def big_forward(k):
        for g in (2 * k, 2 * k + 1):
            ag(g, 1, 0).wait_recv()
            ag(g, 1, 4).start()
        for g in (2 * k, 2 * k + 1):
            ag(g, 1, 2).wait_recv()
            if g % 2 == 0:
                ag(g, 1, 5).start()
            ag(g, 1, 3).start()
            ag(g, 1, 1).start()
        y_source(k, 1)
        y_source(k, 2)

    def big_last(k):
        ag(2 * k, 1, 4).wait_recv()
        ag(2 * k, 1, 5).wait_recv()
        ag(2 * k + 1, 1, 4).wait_recv()
        y_source(k, 3)
        ag(2 * k + 1, 1, 3).wait_recv()
        ag(2 * k + 1, 1, 5).start()

    def big_end(k):
        ag(2 * k, 1, 1).wait_recv()
        ag(2 * k, 1, 3).wait_recv()
        ag(2 * k + 1, 1, 1).wait_recv()
        ag(2 * k + 1, 1, 5).wait_recv()

    y, ys = r // 2, (c % NR) // 2
    chain = side == c % 2
    hop = ((y - ys + 4) % 4, (ys - y + 4) % 4)

    def piece(g, i):
        return ring(g, True)[0] + (0, 3, 1, 2)[i]

    def y_refs(g, i):
        n = piece(g, i) % 4
        if g % 2 == 0:
            return o_refs[g].at[par, :, n], j_refs[g].at[:, n]
        return o_refs[g].at[par, :, :, n], j_refs[g].at[:, :, n]

    def y_copy(g, i, to_twin, from_o):
        o, j = y_refs(g, i)
        step = 2 if g % 2 == 0 else 6
        to = twin if to_twin else (r + step) % NR
        return copy(
            o if from_o else j, j, y_s.at[g, i, to_twin], y_r.at[g, i], (to, c)
        )

    def y_local(g, i):
        o, j = y_refs(g, i)
        return pltpu.make_async_copy(o, j, loc.at[g, i])

    def y_source(k, i):
        for g in (2 * k, 2 * k + 1):

            @pl.when(chain & (hop[g % 2] == 0))
            def _():
                y_copy(g, i, 0, True).start()
                y_copy(g, i, 1, True).start()
                y_local(g, i).start()

    def y_step(k, step):
        for far in (1, 2, 3):
            for g in (2 * k, 2 * k + 1):
                i = step - far
                if 0 <= i < 4:

                    @pl.when(chain & (hop[g % 2] == far))
                    def _():
                        y_copy(g, i, 0, False).wait_recv()
                        if far < 3:
                            y_copy(g, i, 0, False).start()
                        y_copy(g, i, 1, False).start()

    def y_last(k):
        for g in (2 * k, 2 * k + 1):
            for i in range(4):

                @pl.when(jnp.logical_not(chain))
                def _():
                    y_copy(g, i, 0, False).wait_recv()

                @pl.when(chain & (hop[g % 2] == 0))
                def _():
                    y_local(g, i).wait()

                @pl.when(chain & (hop[g % 2] < 3))
                def _():
                    y_copy(g, i, 0, False).wait_send()

                @pl.when(chain)
                def _():
                    y_copy(g, i, 1, False).wait_send()

    done = []

    def f(count):
        for _ in range(count):
            q = len(done)
            done.append(q)
            k, part = q // 8, q % 8
            if q == 0:
                p4().wait_recv()
                build_g(
                    pv2[0].reshape(256, 256), pv2[1].reshape(256, 256),
                    pv2[2].reshape(256, 256), pat_ref[1:2, 0:1].astype(F32), g_ref,
                )
            if part == 0:
                diag_begin(k, g_ref, s_ref)
            panels(s_ref, part * 2, part * 2 + 2)
            if part == 7:
                diag_end(k, g_ref, s_ref, l_ref, v_ref)

    def e0(k):
        for d in range(1, NR):
            a2a(k, d).wait_recv()
        if k == 0:
            lab = labels_in()
        for p in (0, 1):
            if k == 0:
                picks_in(lab, p)
            fill(k, p)
            rs_start(k, 0, p)

    e0(0)
    p4_start()
    e0(1)
    f(3)
    rs_middle(0, 0)
    f(3)
    rs_end(0, 0)
    f(1)
    rs_middle(1, 0)
    f(2)
    rs_middle(0, 1)
    f(2)
    rs_end(0, 1)
    ag_own(0)
    ag_start(0)
    f(2)
    ag_forward(0)
    f(1)
    rs_end(1, 0)
    f(2)
    big_start(0)
    rs_middle(1, 1)
    f(2)
    rs_end(1, 1)
    ag_own(1)
    ag_start(1)
    big_forward(0)
    f(1)
    y_step(0, 1)
    ag_forward(1)
    f(2)
    big_start(1)
    y_step(0, 2)
    f(1)
    big_last(0)
    y_step(0, 3)
    f(1)
    big_forward(1)
    y_step(1, 1)
    y_step(0, 4)
    f(1)
    y_step(0, 5)
    y_step(1, 2)
    f(2)
    big_last(1)
    f(1)
    y_step(0, 6)
    big_end(0)
    y_step(1, 3)
    f(2)
    y_step(1, 4)
    f(2)
    y_step(1, 5)
    f(1)
    y_step(1, 6)
    big_end(1)
    for k in (0, 1):
        y_last(k)

    for g in range(4):
        for phase in (0, 1):
            for m in range(6):
                rs(g, phase, m).wait_send()
                ag(g, phase, m).wait_send()
    for k in (0, 1):
        for d in range(1, NR):
            a2a(k, d).wait_send()
    for b, (sr, sc) in enumerate(sources):

        @pl.when((r == sr) & (c == sc))
        def _():
            for d in range(1, NC):
                p1(b, d).wait_send()

    for k in (0, 1):

        @pl.when(r == k)
        def _():
            for d in range(1, NR):
                p2(k, d).wait_send()

    for d in range(1, NC):
        p3(d).wait_send()
    p4().wait_send()


def move(live, pattern, dest, lrow, coup, blocks):
    vm = pl.BlockSpec(memory_space=pltpu.VMEM)
    sm = pl.BlockSpec(memory_space=pltpu.SMEM)
    hb = pl.BlockSpec(memory_space=pltpu.HBM)
    dma = pltpu.SemaphoreType.DMA
    group = jax.ShapeDtypeStruct((2, 5, NX, NZ, 16, 128), F32)
    cols = jax.ShapeDtypeStruct((5, NX, NZ, 16, 128), F32)
    square = jax.ShapeDtypeStruct((512, 512), F32)
    return pl.pallas_call(
        move_kernel,
        out_shape=(group,) * 4 + (cols,) * 4 + (square, square),
        in_specs=[sm] + [hb] * 5,
        out_specs=[vm] * 10,
        scratch_shapes=[
            pltpu.VMEM((NR, 72, 256), F32),
            pltpu.VMEM((NR, 64, 256), F32),
            pltpu.VMEM((NR, 72, 256), F32),
            pltpu.VMEM((NR, 64, 256), F32),
            pltpu.VMEM((2, 1280, 512), BF),
            pltpu.VMEM((10, 256, 256), BF),
            pltpu.VMEM((3, NC, 16, 256), F32),
            pltpu.VMEM((3, NC, 16, 256), F32),
            pltpu.VMEM((NC, 16, 256), F32),
        ]
        + [pltpu.VMEM((2, 5, NX, NZ, 16, 128), F32)] * 4
        + [pltpu.VMEM((6, 5, 4, 16, 128), F32)] * 4
        + [pltpu.VMEM((6, 5, 16, 128), F32)] * 4
        + [
            pltpu.VMEM((512, 512), F32),
            pltpu.VMEM((128, 256), F32),
            pltpu.VMEM((80, 80), jnp.int32),
            pltpu.VMEM((1, 256), jnp.int32),
            pltpu.VMEM((1, 256), jnp.int32),
            pltpu.VMEM((1024, 128), F32),
            pltpu.VMEM((256, 256), BF),
            dma((2, NR)), dma((2, NR)),
            dma((3, NC)), dma((3,)),
            dma((2, NR)), dma((2,)),
            dma((NC,)), dma((NC,)),
            dma(()), dma(()),
            dma((4, 2, 6)), dma((4, 2, 6)),
            dma((4, 2, 6)), dma((4, 2, 6)),
            dma((4, 4, 2)), dma((4, 4)),
            dma((4, 5)), dma((6,)),
        ],
        compiler_params=pltpu.CompilerParams(
            collective_id=0, has_side_effects=True, vmem_limit_bytes=40 * 1024 * 1024
        ),
        name="move",
    )(live, pattern, dest, lrow, coup, blocks)


def update_kernel(
    where_ref, pat_ref, a0_ref, a1_ref, a2_ref, a3_ref, j0_ref, j1_ref, j2_ref, j3_ref,
    l_ref, v_ref, hess_ref, o_ref, v_s, wj_s,
):
    s = pl.program_id(0)
    r, c = where_ref[0], where_ref[1]

    def wide(left, right):
        return jnp.concatenate([left, right], axis=1)

    def solve(a0, a1):
        h0, l0 = split(a0)
        h1, l1 = split(a1)
        w0 = dot1(jnp.concatenate([h0, l0, h0], 1), v_s[0:256, 0:768], 1, 1)
        w1 = dot1(jnp.concatenate([h0, l0, h0, h1, l1, h1], 1), v_s[256:512, :], 1, 1)
        return w0, w1

    @pl.when(s == 0)
    def _():
        for k in (0, 1):
            hi, lo = split(v_ref[:, k * 256 : (k + 1) * 256])
            v_s[:, k * 768 : (k + 1) * 768] = jnp.concatenate([hi, hi, lo], 1)

        def column(u, carry):
            j = u * NC + c
            w0, w1 = solve(
                wide(j0_ref[u], j1_ref[u]) * pat_ref[j, 0].astype(F32),
                wide(j2_ref[u], j3_ref[u]) * pat_ref[j, 1].astype(F32),
            )
            h0, l0 = split(w0)
            h1, l1 = split(w1)
            wj_s[u] = jnp.concatenate([h0, l0, h0, h1, l1, h1], 1)
            return carry

        lax.fori_loop(0, 5, column, 0)

    rows = (s * 2 * NR + r, s * 2 * NR + NR + r)

    def links(k):
        return jnp.where(
            iota((512, 1), 0) < 256, pat_ref[rows[0], k], pat_ref[rows[1], k]
        ).astype(F32)

    def pair(left, right):
        return wide(left[:, s].reshape(512, 128), right[:, s].reshape(512, 128))

    w0, w1 = solve(pair(a0_ref, a1_ref) * links(0), pair(a2_ref, a3_ref) * links(1))
    h0, l0 = split(w0)
    h1, l1 = split(w1)
    wi = jnp.concatenate([h0, h0, l0, h1, h1, l1], 1)

    def put(p, u, value):
        for h in range(2):
            o_ref[pl.Slice(2560 * p + 2 * u + h, 256, 10), :] = value[:, h * 128 : (h + 1) * 128]

    for u in range(5):
        j = u * NC + c
        panel = j < 2

        @pl.when((u < s) & jnp.logical_not(panel))
        def _():
            upd = dot1(wi, wj_s[u], 1, 1)
            for p in (0, 1):
                tile = hess_ref[2 * s + p, u].astype(F32)
                put(p, u, tile * pat_ref[rows[p], j].astype(F32) - upd[p * 256 : p * 256 + 256])

        for p in (0, 1):
            i = rows[p]

            @pl.when((u == s) & (i >= j) & jnp.logical_not(panel))
            def _():
                tile = hess_ref[2 * s + p, u].astype(F32)
                upd = dot1(wi[p * 256 : p * 256 + 256], wj_s[u], 1, 1)

                @pl.when(i == j)
                def _():
                    put(p, u, sym_block(tile) - upd)

                @pl.when(i != j)
                def _():
                    put(p, u, tile * pat_ref[i, j].astype(F32) - upd)

            @pl.when((i < j) & jnp.logical_not(panel))
            def _():
                put(p, u, jnp.zeros((256, 256), F32))

            if u == 0:

                @pl.when(panel & (i >= 2))
                def _():
                    put(p, u, jnp.where(c == 0, w0, w1)[p * 256 : p * 256 + 256])

                if p == 0:

                    @pl.when(panel & (i < 2))
                    def _():
                        at = pl.ds(pl.multiple_of(i * 256, 256), 256)
                        put(p, u, jnp.where(c == 0, l_ref[at, 0:256], l_ref[at, 256:512]))


def update(where, pattern, moved, hess):
    vm = pl.BlockSpec(memory_space=pltpu.VMEM)
    sm = pl.BlockSpec(memory_space=pltpu.SMEM)
    return pl.pallas_call(
        update_kernel,
        grid=(5,),
        out_shape=jax.ShapeDtypeStruct((25600, 128), F32),
        in_specs=[sm, sm] + [vm] * 11,
        out_specs=pl.BlockSpec((5120, 128), lambda s: (s, 0)),
        scratch_shapes=[pltpu.VMEM((512, 1536), BF), pltpu.VMEM((5, 256, 1536), BF)],
        compiler_params=pltpu.CompilerParams(vmem_limit_bytes=20 * 1024 * 1024),
        name="update",
    )(
        where, pattern, *[o.reshape(2, 5, 256, 128) for o in moved[0:4]],
        *[j.reshape(5, 256, 128) for j in moved[4:8]], *moved[8:], hess,
    )


def shards(hess, coupling, dest_row, local_row, live, pattern):
    blocks = jnp.transpose(hess[:, 0, :, :, 0, :], (0, 2, 1, 3))
    where = jnp.stack([lax.axis_index("row"), lax.axis_index("col")]).astype(jnp.int32)
    coup = jnp.transpose(coupling.reshape(256, 2, 2, 128), (0, 2, 1, 3)).reshape(1024, 128)
    moved = move(
        live, pattern, dest_row.reshape(1, 256), local_row, coup, blocks
    )
    out = update(where, pattern, moved, blocks)
    return out.reshape(10, 1, 256, 5, 1, 256)


def solution(mesh):
    return jax.shard_map(
        shards,
        mesh=mesh,
        in_specs=(
            P(None, "row", None, None, "col", None),
            P(("row", "col"), None, None, None),
            P(("row", "col"), None, None),
            P(("row", "col"), None),
            P(("row", "col")),
            P(),
        ),
        out_specs=P(None, "row", None, None, "col", None),
        check_vma=False,
    )
```

```python
import jax
import jax.numpy as jnp
from jax import lax
from jax.experimental import pallas as pl
from jax.experimental.pallas import tpu as pltpu
from jax.sharding import PartitionSpec as P

F32 = jnp.float32
BF = jnp.bfloat16
MESH = pl.DeviceIdType.MESH
NR, NC, NX, NZ = 8, 16, 4, 4


def dotg(a, b, ca, cb, precision=lax.Precision.HIGHEST):
    return lax.dot_general(
        a, b, (((ca,), (cb,)), ((), ())), precision=precision, preferred_element_type=F32
    )


def dot1(a, b, ca, cb):
    return lax.dot_general(a, b, (((ca,), (cb,)), ((), ())), preferred_element_type=F32)


def split(x):
    hi = x.astype(BF)
    return hi, (x - hi.astype(F32)).astype(BF)


def split3(x):
    hi = x.astype(BF).astype(F32)
    mid = (x - hi).astype(BF).astype(F32)
    return hi, mid, x - hi - mid


def iota(shape, dim):
    return lax.broadcasted_iota(jnp.int32, shape, dim)


def sym_block(x):
    n = x.shape[0]
    return jnp.where(iota((n, n), 0) >= iota((n, n), 1), x, x.T)


def build_g(h00, h10, h11, link, g_ref):
    g_ref[0:256, 0:256] = sym_block(h00)
    g_ref[256:512, 256:512] = sym_block(h11)
    x = h10 * link
    g_ref[256:512, 0:256] = x
    g_ref[0:256, 256:512] = x.T
    for i in range(4):
        rows = slice(i * 128, (i + 1) * 128)
        g = g_ref[rows, :]
        on = iota((128, 512), 0) + i * 128 == iota((128, 512), 1)
        s = jnp.sum(jnp.where(on, 0.0, jnp.abs(g)), axis=1, keepdims=True) + 1.0
        g_ref[rows, :] = jnp.where(on, s, g)


def panels(s_ref, lo, hi):
    lane = iota((8, 128), 1)
    sub = iota((8, 1), 0)

    def body(b, carry):
        base = pl.multiple_of(b * 8, 8)
        rows = s_ref[pl.ds(base, 8), :]
        ra = rows[:, :128]
        cs = [
            jnp.sum(jnp.where(lane == base + j, ra, 0.0), axis=1, keepdims=True)
            for j in range(8)
        ]
        invd = jnp.zeros((8, 1), F32)
        for j in range(8):
            inv = 1.0 / cs[j][j : j + 1, :]
            m = jnp.where(sub > j, cs[j] * inv, 0.0)
            invd = jnp.where(sub == j, inv, invd)
            rows = rows - m * rows[j : j + 1, :]
            for k in range(j + 1, 8):
                cs[k] = cs[k] - m * cs[k][j : j + 1, :]
        s_ref[pl.ds(base, 8), :] = rows
        um = jnp.where(lane >= base + 8, rows[:, :128], 0.0)
        u, w = split3(um), split3(rows * invd)
        left = jnp.concatenate([u[i] for i in (0, 0, 1, 0, 2, 1)], axis=0).astype(BF)
        right = jnp.concatenate([w[i] for i in (0, 1, 0, 2, 0, 1)], axis=0).astype(BF)
        s_ref[...] = s_ref[...] - dot1(left, right, 0, 0)
        return carry

    lax.fori_loop(lo, hi, body, 0)


def diag_begin(k, g_ref, s_ref):
    o = k * 128
    s_ref[:, 0:128] = g_ref[o : o + 128, o : o + 128]
    s_ref[:, 128:256] = jnp.where(iota((128, 128), 0) == iota((128, 128), 1), 1.0, 0.0)


def diag_end(k, g_ref, s_ref, l_ref, v_ref):
    o, e = k * 128, k * 128 + 128
    r, c = iota((128, 128), 0), iota((128, 128), 1)
    u = s_ref[:, 0:128]
    s = lax.rsqrt(jnp.sum(jnp.where(r == c, u, 0.0), axis=1, keepdims=True))
    l_ref[o:e, o:e] = jnp.where(r <= c, u * s, 0.0).T
    v = s_ref[:, 128:256] * s
    v_ref[o:e, o:e] = v
    if e < 512:
        lp = dotg(g_ref[e:512, o:e], v, 1, 1)
        l_ref[e:512, o:e] = lp
        l_ref[o:e, e:512] = jnp.zeros((128, 512 - e), F32)
        v_ref[o:e, e:512] = jnp.zeros((128, 512 - e), F32)
        g_ref[e:512, e:512] = g_ref[e:512, e:512] - dotg(lp, lp, 1, 1)
    if o > 0:
        t = dotg(l_ref[o:e, 0:o], v_ref[0:o, 0:o], 1, 0)
        v_ref[o:e, 0:o] = -dotg(v, t, 1, 0)


def move_kernel(
    live_ref, pat_hbm, dest_hbm, lrow_hbm, coup_hbm, hess_ref, *refs
):
    o_refs, j_refs, refs = refs[0:4], refs[4:8], refs[8:]
    (l_ref, v_ref, pack_s0, pack_s1, pack_r0, pack_r1, picks, hcol_ref, pv, pv2, pv_src), refs = (
        refs[:11],
        refs[11:],
    )
    pack_s, pack_r = (pack_s0, pack_s1), (pack_r0, pack_r1)
    p_refs, first_buf, second_buf, refs = refs[0:4], refs[4:8], refs[8:12], refs[12:]
    g_ref, s_ref, pat_ref, dest_ref, lrow_ref, coup_ref, lead_ref = refs[:7]
    (
        a2a_s, a2a_r, p1_s, p1_r, p2_s, p2_r, p3_s, p3_r, p4_s, p4_r,
        rs_s, rs_r, ag_s, ag_r, y_s, y_r, loc, hload,
    ) = refs[7:]
    r = lax.axis_index("row")
    c = lax.axis_index("col")
    x, z = c // NZ, c % NZ
    side = r % 2
    twin = r + 1 - 2 * side
    par = c // NR

    def copy(src, dst, ss, rs, dev):
        return pltpu.make_async_remote_copy(
            src_ref=src, dst_ref=dst, send_sem=ss, recv_sem=rs, device_id=dev,
            device_id_type=MESH,
        )

    barrier = pltpu.get_barrier_semaphore()
    for d in range(1, NR):
        pl.semaphore_signal(barrier, 1, device_id=((r + d) % NR, c), device_id_type=MESH)
    for d in range(1, NC):
        pl.semaphore_signal(barrier, 1, device_id=(r, (c + d) % NC), device_id_type=MESH)
    loads = [
        pltpu.make_async_copy(src, dst, hload.at[i])
        for i, (src, dst) in enumerate(
            (
                (dest_hbm, dest_ref),
                (lrow_hbm, lrow_ref),
                (coup_hbm, coup_ref),
                (hess_ref.at[0, 0], lead_ref),
                (pat_hbm, pat_ref),
                (hess_ref.at[:, 0], hcol_ref),
            )
        )
    ]
    for load in loads:
        load.start()
    for load in loads[:4]:
        load.wait()

    lane = iota((1, 256), 1)
    active = lane < live_ref[0]
    dest = dest_ref[...]
    hits = jnp.where((iota((NR, 256), 0) == dest) & active, 1.0, 0.0)
    before = jnp.where(iota((256, 256), 0) <= iota((256, 256), 1), 1.0, 0.0).astype(BF)
    cum = dot1(hits.astype(BF), before, 1, 0)
    rank = jnp.sum(hits * cum, axis=0, keepdims=True).astype(jnp.int32) - 1
    place = jnp.where(active, dest * 64 + rank, -1)
    pick = jnp.where(iota((512, 256), 0) == place, 1.0, 0.0).astype(BF)
    lr = lrow_ref[...]
    spot = jnp.where(iota((512, 256), 0) == rank + r * 64, 1.0, 0.0).astype(BF)
    lab_hi = (hits * (lr // 256).astype(F32)).astype(BF)
    lab_lo = (hits * (lr % 256).astype(F32)).astype(BF)
    labels = (
        dot1(lab_hi, spot, 1, 1) * 256.0
        + dot1(lab_lo, spot, 1, 1)
        + dot1(hits.astype(BF), spot, 1, 1)
    )
    for g in range(NR):
        pack_s[0][g, 64:72, :] = jnp.where(
            iota((8, 256), 0) == 0, labels[g : g + 1, 0:256], labels[g : g + 1, 256:512]
        )

    def pack(k):
        rows = jnp.concatenate(
            [coup_ref[pl.Slice(2 * h + k, 256, 4), :] for h in range(2)], axis=1
        )
        c_hi, c_lo = split(rows)
        packed = dot1(pick, c_hi, 1, 0) + dot1(pick, c_lo, 1, 0)
        pack_s[k][:, 0:64, :] = packed.reshape(NR, 64, 256)

    def a2a(k, d):
        to = (r + d) % NR
        return copy(
            pack_s[k].at[to], pack_r[k].at[r], a2a_s.at[k, d], a2a_r.at[k, d], (to, c)
        )

    far_first = (4, 3, 5, 2, 6, 1, 7)
    pv_src[...] = lead_ref[...].astype(F32).reshape(NC, 16, 256)
    pack(0)
    pl.semaphore_wait(barrier, NR - 1 + NC - 1)

    sources = ((0, 0), (1, 0), (1, 1))

    def p1(b, d):
        to = (sources[b][1] + d) % NC
        return copy(pv_src.at[to], pv.at[b, to], p1_s.at[b, d], p1_r.at[b], (sources[b][0], to))

    for b, (sr, sc) in enumerate(sources):

        @pl.when((r == sr) & (c == sc))
        def _():
            for d in range(1, NC):
                p1(b, d).start()
            pv[b, sc] = pv_src[sc]

    for d in far_first:
        a2a(0, d).start()
    pack_r[0][r] = pack_s[0][r]
    pack(1)

    def p2(k, d):
        blocks = pl.ds(0, 1) if k == 0 else pl.ds(1, 2)
        to = (k + d) % NR
        part = pv.at[blocks, c]
        return copy(part, part, p2_s.at[k, d], p2_r.at[k], (to, c))

    def p2_start():
        for b, (sr, sc) in enumerate(sources):

            @pl.when((r == sr) & (c != sc))
            def _():
                p1(b, 1).wait_recv()

        for k in (0, 1):

            @pl.when(r == k)
            def _():
                for d in range(1, NR):
                    p2(k, d).start()

    eight = pl.ds(pl.multiple_of(8 * side, 8), 8)

    def p3(d):
        return copy(
            pv.at[:, c, eight], pv2.at[:, c, eight], p3_s.at[d], p3_r.at[d], (r, (c + d) % NC)
        )

    def p3_start():
        for k in (0, 1):

            @pl.when(r != k)
            def _():
                p2(k, 1).wait_recv()

        for d in range(1, NC):
            p3(d).start()
        pv2[:, c, eight] = pv[:, c, eight]

    def p4():
        part = pv2.at[:, :, eight]
        return copy(part, part, p4_s, p4_r, (twin, c))

    def p4_start():
        for d in range(1, NC):
            p3(d).wait_recv()
        p4().start()

    p2_start()
    for d in far_first:
        a2a(1, d).start()
    pack_r[1][r] = pack_s[1][r]
    p3_start()
    loads[4].wait()
    loads[5].wait()

    def labels_in():
        lab = jnp.zeros((8, 256), F32)
        for g in range(NR):
            lab = lab + pack_r[0][g, 64:72, :]
        return jnp.concatenate([lab[0:1], lab[1:2]], axis=1).astype(jnp.int32) - 1

    def picks_in(lab, p):
        for t2 in range(5):
            t = 2 * t2 + p
            pick = jnp.where(iota((256, 512), 0) + t * 256 == lab, 1.0, 0.0).astype(BF)
            picks[p, t2 * 256 : t2 * 256 + 256, :] = pick

    def fill(k, p):
        rows = jnp.concatenate([pack_r[k][g, 0:64, :] for g in range(NR)], axis=0)
        hi, lo = split(rows)
        mine = jnp.where(c == k, 1.0, 0.0)
        got = dot1(picks[p], hi, 1, 0) + dot1(picks[p], lo, 1, 0)
        for t2 in range(5):
            part = got[t2 * 256 : t2 * 256 + 256] + hcol_ref[2 * t2 + p].astype(F32) * mine
            for h in range(2):
                p_refs[2 * k + h][p, t2] = part[:, h * 128 : (h + 1) * 128].reshape(
                    NX, NZ, 16, 128
                )

    def along_x(n):
        return (r, (n % NX) * NZ + z)

    def along_z(n):
        return (r, x * NZ + n % NZ)

    def unit(ref, g, big, n, p):
        n = n % 4
        if g % 2 == 0:
            return ref.at[p, :, n] if big else ref.at[p, :, x, n]
        return ref.at[p, :, :, n] if big else ref.at[p, :, n, z]

    def ring(g, big):
        return (x, along_x) if (g % 2 == 0) == big else (z, along_z)

    def rs(g, phase, m):
        n, dev = ring(g, phase == 0)
        buf = (first_buf, second_buf)[phase][g]
        at, p, to = (
            (n + 2, 0, n + 1), (n + 1, 1, n + 1), (n + 1, 0, n + 1),
            (n + 2, 1, n + 3), (n + 3, 0, n + 3), (n + 3, 1, n + 3),
        )[m]
        return copy(
            unit(p_refs[g], g, phase == 0, at, p), buf.at[m],
            rs_s.at[g, phase, m], rs_r.at[g, phase, m], dev(to),
        )

    def rs_start(k, phase, p):
        for m in ((0, 4), (3, 1))[p]:
            for g in (2 * k, 2 * k + 1):
                rs(g, phase, m).start()

    def rs_middle(k, phase):
        for m_in, m_out, step, p in ((0, 2, 1, 0), (3, 5, 3, 1)):
            for g in (2 * k, 2 * k + 1):
                n, dev = ring(g, phase == 0)
                rs(g, phase, m_in).wait_recv()
                ref = unit(p_refs[g], g, phase == 0, n + step, p)
                ref[...] = ref[...] + (first_buf, second_buf)[phase][g][m_in]
                rs(g, phase, m_out).start()

    def rs_end(k, phase):
        for p, (m1, m2) in enumerate(((4, 2), (1, 5))):
            for g in (2 * k, 2 * k + 1):
                n, dev = ring(g, phase == 0)
                buf = (first_buf, second_buf)[phase][g]
                rs(g, phase, m1).wait_recv()
                rs(g, phase, m2).wait_recv()
                ref = unit(p_refs[g], g, phase == 0, n, p)
                ref[...] = ref[...] + (buf[m1] + buf[m2])
            if phase == 0:
                rs_start(k, 1, p)

    def ag(g, phase, m):
        n, dev = ring(g, phase == 1)
        want = (lambda i: 0) if phase == 0 else (lambda i: i % 4 // 2) if g % 2 == 0 else (lambda i: par)
        back = want(n) if phase == 1 and g % 2 == 0 else 1 - want(n)
        at, p, to = (
            (n, want(n + 1), n + 1), (n, 1 - want(n + 1), n + 1), (n, want(n + 3), n + 3),
            (n, 1 - want(n + 3), n + 3), (n + 3, want(n), n + 1), (n + 1, back, n + 3),
        )[m]
        src = unit(o_refs[g], g, phase == 1, at, p)
        return copy(src, src, ag_s.at[g, phase, m], ag_r.at[g, phase, m], dev(to))

    def ag_own(k):
        keeps = [
            pltpu.make_async_copy(
                p_refs[g].at[:, :, x, z], o_refs[g].at[:, :, x, z], loc.at[g, 4]
            )
            for g in (2 * k, 2 * k + 1)
        ]
        for keep in keeps:
            keep.start()
        for keep in keeps:
            keep.wait()

    def ag_start(k):
        for m in (0, 3, 1, 2):
            for g in (2 * k, 2 * k + 1):
                ag(g, 0, m).start()

    def ag_forward(k):
        for m_in, m_out in ((0, 4), (3, 5)):
            for g in (2 * k, 2 * k + 1):
                ag(g, 0, m_in).wait_recv()
                ag(g, 0, m_out).start()

    def big_start(k):
        for m in (1, 2, 4, 5):
            for g in (2 * k, 2 * k + 1):
                ag(g, 0, m).wait_recv()
        for m in (0, 2):
            for g in (2 * k, 2 * k + 1):
                ag(g, 1, m).start()
        y_source(k, 0)

    def big_forward(k):
        for g in (2 * k, 2 * k + 1):
            ag(g, 1, 0).wait_recv()
            ag(g, 1, 4).start()
        for g in (2 * k, 2 * k + 1):
            ag(g, 1, 2).wait_recv()
            if g % 2 == 0:
                ag(g, 1, 5).start()
            ag(g, 1, 3).start()
            ag(g, 1, 1).start()
        y_source(k, 1)
        y_source(k, 2)

    def big_last(k):
        ag(2 * k, 1, 4).wait_recv()
        ag(2 * k, 1, 5).wait_recv()
        ag(2 * k + 1, 1, 4).wait_recv()
        y_source(k, 3)
        ag(2 * k + 1, 1, 3).wait_recv()
        ag(2 * k + 1, 1, 5).start()

    def big_end(k):
        ag(2 * k, 1, 1).wait_recv()
        ag(2 * k, 1, 3).wait_recv()
        ag(2 * k + 1, 1, 1).wait_recv()
        ag(2 * k + 1, 1, 5).wait_recv()

    y, ys = r // 2, (c % NR) // 2
    chain = side == c % 2
    hop = (y - ys + 4) % 4

    def piece(g, i):
        return ring(g, True)[0] + (0, 3, 1, 2)[i]

    def y_refs(g, i):
        n = piece(g, i) % 4
        if g % 2 == 0:
            return o_refs[g].at[par, :, n], j_refs[g].at[:, n]
        return o_refs[g].at[par, :, :, n], j_refs[g].at[:, :, n]

    def y_copy(g, i, way, from_o=False):
        o, j = y_refs(g, i)
        onward = 2 if g % 2 == 0 else 6
        to = ((r + 2) % NR, twin, (r + 6) % NR, (r + onward) % NR)[way]
        return copy(o if from_o else j, j, y_s.at[g, i, way], y_r.at[g, i], (to, c))

    def y_local(g, i):
        o, j = y_refs(g, i)
        return pltpu.make_async_copy(o, j, loc.at[g, i])

    def y_source(k, i):
        @pl.when(chain & (hop == 0))
        def _():
            for g in (2 * k, 2 * k + 1):
                for way in ((0, 2), (2, 0))[g % 2]:
                    y_copy(g, i, way, True).start()
            for g in (2 * k, 2 * k + 1):
                y_copy(g, i, 1, True).start()
                y_local(g, i).start()

    def near(k, i):
        for far in (1, 3):

            @pl.when(chain & (hop == far))
            def _():
                for g in (2 * k, 2 * k + 1) if far == 1 else (2 * k + 1, 2 * k):
                    y_copy(g, i, 1).wait_recv()
                    if (far == 1) == (g % 2 == 0):
                        y_copy(g, i, 3).start()
                    y_copy(g, i, 1).start()

    def far(k, i):
        @pl.when(chain & (hop == 2))
        def _():
            for g in (2 * k, 2 * k + 1):
                y_copy(g, i, 1).wait_recv()
                y_copy(g, i, 1).start()

    def y_last(k):
        for g in (2 * k, 2 * k + 1):
            for i in range(4):

                @pl.when(jnp.logical_not(chain))
                def _():
                    y_copy(g, i, 1).wait_recv()

                @pl.when(chain & (hop == 0))
                def _():
                    y_local(g, i).wait()
                    y_copy(g, i, 0).wait_send()
                    y_copy(g, i, 2).wait_send()

                @pl.when(chain & (hop == (1 if g % 2 == 0 else 3)))
                def _():
                    y_copy(g, i, 3).wait_send()

                @pl.when(chain)
                def _():
                    y_copy(g, i, 1).wait_send()

    done = []

    def f(count):
        for _ in range(count):
            q = len(done)
            done.append(q)
            k, part = q // 8, q % 8
            if q == 0:
                p4().wait_recv()
                build_g(
                    pv2[0].reshape(256, 256), pv2[1].reshape(256, 256),
                    pv2[2].reshape(256, 256), pat_ref[1:2, 0:1].astype(F32), g_ref,
                )
            if part == 0:
                diag_begin(k, g_ref, s_ref)
            panels(s_ref, part * 2, part * 2 + 2)
            if part == 7:
                diag_end(k, g_ref, s_ref, l_ref, v_ref)

    def e0(k):
        for d in range(1, NR):
            a2a(k, d).wait_recv()
        if k == 0:
            lab = labels_in()
        for p in (0, 1):
            if k == 0:
                picks_in(lab, p)
            fill(k, p)
            rs_start(k, 0, p)

    e0(0)
    p4_start()
    e0(1)
    f(4)
    rs_middle(0, 0)
    f(4)
    rs_end(0, 0)
    f(1)
    rs_middle(1, 0)
    f(2)
    rs_middle(0, 1)
    f(2)
    rs_end(0, 1)
    ag_own(0)
    ag_start(0)
    f(2)
    ag_forward(0)
    f(1)
    rs_end(1, 0)
    f(2)
    big_start(0)
    rs_middle(1, 1)
    f(2)
    rs_end(1, 1)
    ag_own(1)
    ag_start(1)
    big_forward(0)
    f(2)
    near(0, 0)
    ag_forward(1)
    f(2)
    big_start(1)
    far(0, 0)
    near(0, 1)
    f(1)
    big_last(0)
    near(0, 2)
    f(1)
    big_forward(1)
    far(0, 1)
    near(1, 0)
    f(1)
    near(0, 3)
    far(0, 2)
    f(1)
    big_last(1)
    far(0, 3)
    far(1, 0)
    near(1, 1)
    f(1)
    big_end(0)
    near(1, 2)
    f(1)
    far(1, 1)
    near(1, 3)
    f(2)
    far(1, 2)
    big_end(1)
    far(1, 3)
    for k in (0, 1):
        y_last(k)

    for g in range(4):
        for phase in (0, 1):
            for m in range(6):
                rs(g, phase, m).wait_send()
                ag(g, phase, m).wait_send()
    for k in (0, 1):
        for d in range(1, NR):
            a2a(k, d).wait_send()
    for b, (sr, sc) in enumerate(sources):

        @pl.when((r == sr) & (c == sc))
        def _():
            for d in range(1, NC):
                p1(b, d).wait_send()

    for k in (0, 1):

        @pl.when(r == k)
        def _():
            for d in range(1, NR):
                p2(k, d).wait_send()

    for d in range(1, NC):
        p3(d).wait_send()
    p4().wait_send()


def move(live, pattern, dest, lrow, coup, blocks):
    vm = pl.BlockSpec(memory_space=pltpu.VMEM)
    sm = pl.BlockSpec(memory_space=pltpu.SMEM)
    hb = pl.BlockSpec(memory_space=pltpu.HBM)
    dma = pltpu.SemaphoreType.DMA
    group = jax.ShapeDtypeStruct((2, 5, NX, NZ, 16, 128), F32)
    cols = jax.ShapeDtypeStruct((5, NX, NZ, 16, 128), F32)
    square = jax.ShapeDtypeStruct((512, 512), F32)
    return pl.pallas_call(
        move_kernel,
        out_shape=(group,) * 4 + (cols,) * 4 + (square, square),
        in_specs=[sm] + [hb] * 5,
        out_specs=[vm] * 10,
        scratch_shapes=[
            pltpu.VMEM((NR, 72, 256), F32),
            pltpu.VMEM((NR, 64, 256), F32),
            pltpu.VMEM((NR, 72, 256), F32),
            pltpu.VMEM((NR, 64, 256), F32),
            pltpu.VMEM((2, 1280, 512), BF),
            pltpu.VMEM((10, 256, 256), BF),
            pltpu.VMEM((3, NC, 16, 256), F32),
            pltpu.VMEM((3, NC, 16, 256), F32),
            pltpu.VMEM((NC, 16, 256), F32),
        ]
        + [pltpu.VMEM((2, 5, NX, NZ, 16, 128), F32)] * 4
        + [pltpu.VMEM((6, 5, 4, 16, 128), F32)] * 4
        + [pltpu.VMEM((6, 5, 16, 128), F32)] * 4
        + [
            pltpu.VMEM((512, 512), F32),
            pltpu.VMEM((128, 256), F32),
            pltpu.VMEM((80, 80), jnp.int32),
            pltpu.VMEM((1, 256), jnp.int32),
            pltpu.VMEM((1, 256), jnp.int32),
            pltpu.VMEM((1024, 128), F32),
            pltpu.VMEM((256, 256), BF),
            dma((2, NR)), dma((2, NR)),
            dma((3, NC)), dma((3,)),
            dma((2, NR)), dma((2,)),
            dma((NC,)), dma((NC,)),
            dma(()), dma(()),
            dma((4, 2, 6)), dma((4, 2, 6)),
            dma((4, 2, 6)), dma((4, 2, 6)),
            dma((4, 4, 4)), dma((4, 4)),
            dma((4, 5)), dma((6,)),
        ],
        compiler_params=pltpu.CompilerParams(
            collective_id=0, has_side_effects=True, vmem_limit_bytes=40 * 1024 * 1024
        ),
        name="move",
    )(live, pattern, dest, lrow, coup, blocks)


def update_kernel(
    where_ref, pat_ref, a0_ref, a1_ref, a2_ref, a3_ref, j0_ref, j1_ref, j2_ref, j3_ref,
    l_ref, v_ref, hess_ref, o_ref, v_s, wj_s,
):
    s = pl.program_id(0)
    r, c = where_ref[0], where_ref[1]

    def wide(left, right):
        return jnp.concatenate([left, right], axis=1)

    def solve(a0, a1):
        h0, l0 = split(a0)
        h1, l1 = split(a1)
        w0 = dot1(jnp.concatenate([h0, l0, h0], 1), v_s[0:256, 0:768], 1, 1)
        w1 = dot1(jnp.concatenate([h0, l0, h0, h1, l1, h1], 1), v_s[256:512, :], 1, 1)
        return w0, w1

    @pl.when(s == 0)
    def _():
        for k in (0, 1):
            hi, lo = split(v_ref[:, k * 256 : (k + 1) * 256])
            v_s[:, k * 768 : (k + 1) * 768] = jnp.concatenate([hi, hi, lo], 1)

        def masks(k):
            out = jnp.zeros((1280, 1), F32)
            for u in range(5):
                out = jnp.where(
                    iota((1280, 1), 0) // 256 == u, pat_ref[u * NC + c, k].astype(F32), out
                )
            return out

        def tall(left, right):
            return wide(left[...].reshape(1280, 128), right[...].reshape(1280, 128))

        w0, w1 = solve(tall(j0_ref, j1_ref) * masks(0), tall(j2_ref, j3_ref) * masks(1))
        h0, l0 = split(w0)
        h1, l1 = split(w1)
        wj_s[...] = jnp.concatenate([h0, l0, h0, h1, l1, h1], 1).reshape(5, 256, 1536)

    rows = (s * 2 * NR + r, s * 2 * NR + NR + r)

    def links(k):
        return jnp.where(
            iota((512, 1), 0) < 256, pat_ref[rows[0], k], pat_ref[rows[1], k]
        ).astype(F32)

    def pair(left, right):
        return wide(left[:, s].reshape(512, 128), right[:, s].reshape(512, 128))

    w0, w1 = solve(pair(a0_ref, a1_ref) * links(0), pair(a2_ref, a3_ref) * links(1))
    h0, l0 = split(w0)
    h1, l1 = split(w1)
    wi = jnp.concatenate([h0, h0, l0, h1, h1, l1], 1)

    def put(p, u, value):
        for h in range(2):
            o_ref[pl.Slice(2560 * p + 2 * u + h, 256, 10), :] = value[:, h * 128 : (h + 1) * 128]

    for u in range(5):
        j = u * NC + c
        panel = j < 2

        @pl.when((u < s) & jnp.logical_not(panel))
        def _():
            upd = dot1(wi, wj_s[u], 1, 1)
            for p in (0, 1):
                tile = hess_ref[2 * s + p, u].astype(F32)
                put(p, u, tile * pat_ref[rows[p], j].astype(F32) - upd[p * 256 : p * 256 + 256])

        for p in (0, 1):
            i = rows[p]

            @pl.when((u == s) & (i >= j) & jnp.logical_not(panel))
            def _():
                tile = hess_ref[2 * s + p, u].astype(F32)
                upd = dot1(wi[p * 256 : p * 256 + 256], wj_s[u], 1, 1)

                @pl.when(i == j)
                def _():
                    put(p, u, sym_block(tile) - upd)

                @pl.when(i != j)
                def _():
                    put(p, u, tile * pat_ref[i, j].astype(F32) - upd)

            @pl.when((i < j) & jnp.logical_not(panel))
            def _():
                put(p, u, jnp.zeros((256, 256), F32))

            if u == 0:

                @pl.when(panel & (i >= 2))
                def _():
                    put(p, u, jnp.where(c == 0, w0, w1)[p * 256 : p * 256 + 256])

                if p == 0:

                    @pl.when(panel & (i < 2))
                    def _():
                        at = pl.ds(pl.multiple_of(i * 256, 256), 256)
                        put(p, u, jnp.where(c == 0, l_ref[at, 0:256], l_ref[at, 256:512]))


def update(where, pattern, moved, hess):
    vm = pl.BlockSpec(memory_space=pltpu.VMEM)
    sm = pl.BlockSpec(memory_space=pltpu.SMEM)
    return pl.pallas_call(
        update_kernel,
        grid=(5,),
        out_shape=jax.ShapeDtypeStruct((25600, 128), F32),
        in_specs=[sm, sm] + [vm] * 11,
        out_specs=pl.BlockSpec((5120, 128), lambda s: (s, 0)),
        scratch_shapes=[pltpu.VMEM((512, 1536), BF), pltpu.VMEM((5, 256, 1536), BF)],
        compiler_params=pltpu.CompilerParams(vmem_limit_bytes=30 * 1024 * 1024),
        name="update",
    )(
        where, pattern, *[o.reshape(2, 5, 256, 128) for o in moved[0:4]],
        *[j.reshape(5, 256, 128) for j in moved[4:8]], *moved[8:], hess,
    )


def shards(hess, coupling, dest_row, local_row, live, pattern):
    blocks = jnp.transpose(hess[:, 0, :, :, 0, :], (0, 2, 1, 3))
    where = jnp.stack([lax.axis_index("row"), lax.axis_index("col")]).astype(jnp.int32)
    coup = jnp.transpose(coupling.reshape(256, 2, 2, 128), (0, 2, 1, 3)).reshape(1024, 128)
    moved = move(
        live, pattern, dest_row.reshape(1, 256), local_row, coup, blocks
    )
    out = update(where, pattern, moved, blocks)
    return out.reshape(10, 1, 256, 5, 1, 256)


def solution(mesh):
    return jax.shard_map(
        shards,
        mesh=mesh,
        in_specs=(
            P(None, "row", None, None, "col", None),
            P(("row", "col"), None, None, None),
            P(("row", "col"), None, None),
            P(("row", "col"), None),
            P(("row", "col")),
            P(),
        ),
        out_specs=P(None, "row", None, None, "col", None),
        check_vma=False,
    )
```

```python
import jax
import jax.numpy as jnp
from jax import lax
from jax.experimental import pallas as pl
from jax.experimental.pallas import tpu as pltpu
from jax.sharding import PartitionSpec as P

F32 = jnp.float32
BF = jnp.bfloat16
MESH = pl.DeviceIdType.MESH
NR, NC, NX, NZ = 8, 16, 4, 4


def dotg(a, b, ca, cb, precision=lax.Precision.HIGHEST):
    return lax.dot_general(
        a, b, (((ca,), (cb,)), ((), ())), precision=precision, preferred_element_type=F32
    )


def dot1(a, b, ca, cb):
    return lax.dot_general(a, b, (((ca,), (cb,)), ((), ())), preferred_element_type=F32)


def split(x):
    hi = x.astype(BF)
    return hi, (x - hi.astype(F32)).astype(BF)


def split3(x):
    hi = x.astype(BF).astype(F32)
    mid = (x - hi).astype(BF).astype(F32)
    return hi, mid, x - hi - mid


def iota(shape, dim):
    return lax.broadcasted_iota(jnp.int32, shape, dim)


def sym_block(x):
    n = x.shape[0]
    return jnp.where(iota((n, n), 0) >= iota((n, n), 1), x, x.T)


def build_g(h00, h10, h11, link, g_ref):
    g_ref[0:256, 0:256] = sym_block(h00)
    g_ref[256:512, 256:512] = sym_block(h11)
    x = h10 * link
    g_ref[256:512, 0:256] = x
    g_ref[0:256, 256:512] = x.T
    for i in range(4):
        rows = slice(i * 128, (i + 1) * 128)
        g = g_ref[rows, :]
        on = iota((128, 512), 0) + i * 128 == iota((128, 512), 1)
        s = jnp.sum(jnp.where(on, 0.0, jnp.abs(g)), axis=1, keepdims=True) + 1.0
        g_ref[rows, :] = jnp.where(on, s, g)


def panels(s_ref, lo, hi):
    lane = iota((8, 128), 1)
    sub = iota((8, 1), 0)

    def body(b, carry):
        base = pl.multiple_of(b * 8, 8)
        rows = s_ref[pl.ds(base, 8), :]
        ra = rows[:, :128]
        cs = [
            jnp.sum(jnp.where(lane == base + j, ra, 0.0), axis=1, keepdims=True)
            for j in range(8)
        ]
        invd = jnp.zeros((8, 1), F32)
        for j in range(8):
            inv = 1.0 / cs[j][j : j + 1, :]
            m = jnp.where(sub > j, cs[j] * inv, 0.0)
            invd = jnp.where(sub == j, inv, invd)
            rows = rows - m * rows[j : j + 1, :]
            for k in range(j + 1, 8):
                cs[k] = cs[k] - m * cs[k][j : j + 1, :]
        s_ref[pl.ds(base, 8), :] = rows
        um = jnp.where(lane >= base + 8, rows[:, :128], 0.0)
        u, w = split3(um), split3(rows * invd)
        left = jnp.concatenate([u[i] for i in (0, 0, 1, 0, 2, 1)], axis=0).astype(BF)
        right = jnp.concatenate([w[i] for i in (0, 1, 0, 2, 0, 1)], axis=0).astype(BF)
        s_ref[...] = s_ref[...] - dot1(left, right, 0, 0)
        return carry

    lax.fori_loop(lo, hi, body, 0)


def diag_begin(k, g_ref, s_ref):
    o = k * 128
    s_ref[:, 0:128] = g_ref[o : o + 128, o : o + 128]
    s_ref[:, 128:256] = jnp.where(iota((128, 128), 0) == iota((128, 128), 1), 1.0, 0.0)


def diag_end(k, g_ref, s_ref, l_ref, v_ref):
    o, e = k * 128, k * 128 + 128
    r, c = iota((128, 128), 0), iota((128, 128), 1)
    u = s_ref[:, 0:128]
    s = lax.rsqrt(jnp.sum(jnp.where(r == c, u, 0.0), axis=1, keepdims=True))
    l_ref[o:e, o:e] = jnp.where(r <= c, u * s, 0.0).T
    v = s_ref[:, 128:256] * s
    v_ref[o:e, o:e] = v
    if e < 512:
        lp = dotg(g_ref[e:512, o:e], v, 1, 1)
        l_ref[e:512, o:e] = lp
        l_ref[o:e, e:512] = jnp.zeros((128, 512 - e), F32)
        v_ref[o:e, e:512] = jnp.zeros((128, 512 - e), F32)
        g_ref[e:512, e:512] = g_ref[e:512, e:512] - dotg(lp, lp, 1, 1)
    if o > 0:
        t = dotg(l_ref[o:e, 0:o], v_ref[0:o, 0:o], 1, 0)
        v_ref[o:e, 0:o] = -dotg(v, t, 1, 0)


def move_kernel(
    live_ref, pat_hbm, dest_ref, lrow_ref, coup_ref, hess_ref, *refs
):
    o_refs, j_refs, refs = refs[0:4], refs[4:8], refs[8:]
    (l_ref, v_ref, pack_s0, pack_s1, pack_r0, pack_r1, picks, hcol_ref, pv, pv2, pv_src), refs = (
        refs[:11],
        refs[11:],
    )
    pack_s, pack_r = (pack_s0, pack_s1), (pack_r0, pack_r1)
    p_refs, first_buf, second_buf, refs = refs[0:4], refs[4:8], refs[8:12], refs[12:]
    g_ref, s_ref, pat_ref, lead_ref = refs[:4]
    (
        a2a_s, a2a_r, p1_s, p1_r, p2_s, p2_r, p3_s, p3_r, p4_s, p4_r,
        rs_s, rs_r, ag_s, ag_r, y_s, y_r, loc, hload,
    ) = refs[4:]
    r = lax.axis_index("row")
    c = lax.axis_index("col")
    x, z = c // NZ, c % NZ
    side = r % 2
    twin = r + 1 - 2 * side
    par = c // NR

    def copy(src, dst, ss, rs, dev):
        return pltpu.make_async_remote_copy(
            src_ref=src, dst_ref=dst, send_sem=ss, recv_sem=rs, device_id=dev,
            device_id_type=MESH,
        )

    barrier = pltpu.get_barrier_semaphore()
    for d in range(1, NR):
        pl.semaphore_signal(barrier, 1, device_id=((r + d) % NR, c), device_id_type=MESH)
    for d in range(1, NC):
        pl.semaphore_signal(barrier, 1, device_id=(r, (c + d) % NC), device_id_type=MESH)
    loads = [
        pltpu.make_async_copy(src, dst, hload.at[i])
        for i, (src, dst) in enumerate(
            (
                (hess_ref.at[0, 0], lead_ref),
                (pat_hbm, pat_ref),
                (hess_ref.at[:, 0], hcol_ref),
            )
        )
    ]
    for load in loads:
        load.start()

    lane = iota((1, 256), 1)
    active = lane < live_ref[0]
    dest = dest_ref[...]
    hits = jnp.where((iota((NR, 256), 0) == dest) & active, 1.0, 0.0)
    before = jnp.where(iota((256, 256), 0) <= iota((256, 256), 1), 1.0, 0.0).astype(BF)
    cum = dot1(hits.astype(BF), before, 1, 0)
    rank = jnp.sum(hits * cum, axis=0, keepdims=True).astype(jnp.int32) - 1
    place = jnp.where(active, dest * 64 + rank, -1)
    pick = jnp.where(iota((512, 256), 0) == place, 1.0, 0.0).astype(BF)
    lr = lrow_ref[...]
    spot = jnp.where(iota((512, 256), 0) == rank + r * 64, 1.0, 0.0).astype(BF)
    lab_hi = (hits * (lr // 256).astype(F32)).astype(BF)
    lab_lo = (hits * (lr % 256).astype(F32)).astype(BF)
    labels = (
        dot1(lab_hi, spot, 1, 1) * 256.0
        + dot1(lab_lo, spot, 1, 1)
        + dot1(hits.astype(BF), spot, 1, 1)
    )
    for g in range(NR):
        pack_s[0][g, 64:72, :] = jnp.where(
            iota((8, 256), 0) == 0, labels[g : g + 1, 0:256], labels[g : g + 1, 256:512]
        )

    def pack(k):
        rows = jnp.concatenate(
            [coup_ref[pl.Slice(2 * h + k, 256, 4), :] for h in range(2)], axis=1
        )
        c_hi, c_lo = split(rows)
        packed = dot1(pick, c_hi, 1, 0) + dot1(pick, c_lo, 1, 0)
        pack_s[k][:, 0:64, :] = packed.reshape(NR, 64, 256)

    def a2a(k, d):
        to = (r + d) % NR
        return copy(
            pack_s[k].at[to], pack_r[k].at[r], a2a_s.at[k, d], a2a_r.at[k, d], (to, c)
        )

    far_first = (4, 3, 5, 2, 6, 1, 7)
    pack(0)
    loads[0].wait()
    pv_src[...] = lead_ref[...].astype(F32).reshape(NC, 16, 256)
    pl.semaphore_wait(barrier, NR - 1 + NC - 1)

    sources = ((0, 0), (1, 0), (1, 1))

    def p1(b, d):
        to = (sources[b][1] + d) % NC
        return copy(pv_src.at[to], pv.at[b, to], p1_s.at[b, d], p1_r.at[b], (sources[b][0], to))

    for b, (sr, sc) in enumerate(sources):

        @pl.when((r == sr) & (c == sc))
        def _():
            for d in range(1, NC):
                p1(b, d).start()
            pv[b, sc] = pv_src[sc]

    for d in far_first:
        a2a(0, d).start()
    pack_r[0][r] = pack_s[0][r]
    pack(1)

    def p2(k, d):
        blocks = pl.ds(0, 1) if k == 0 else pl.ds(1, 2)
        to = (k + d) % NR
        part = pv.at[blocks, c]
        return copy(part, part, p2_s.at[k, d], p2_r.at[k], (to, c))

    def p2_start():
        for b, (sr, sc) in enumerate(sources):

            @pl.when((r == sr) & (c != sc))
            def _():
                p1(b, 1).wait_recv()

        for k in (0, 1):

            @pl.when(r == k)
            def _():
                for d in range(1, NR):
                    p2(k, d).start()

    eight = pl.ds(pl.multiple_of(8 * side, 8), 8)

    def p3(d):
        return copy(
            pv.at[:, c, eight], pv2.at[:, c, eight], p3_s.at[d], p3_r.at[d], (r, (c + d) % NC)
        )

    def p3_start():
        for k in (0, 1):

            @pl.when(r != k)
            def _():
                p2(k, 1).wait_recv()

        for d in range(1, NC):
            p3(d).start()
        pv2[:, c, eight] = pv[:, c, eight]

    def p4():
        part = pv2.at[:, :, eight]
        return copy(part, part, p4_s, p4_r, (twin, c))

    def p4_start():
        for d in range(1, NC):
            p3(d).wait_recv()
        p4().start()

    p2_start()
    for d in far_first:
        a2a(1, d).start()
    pack_r[1][r] = pack_s[1][r]
    p3_start()
    loads[1].wait()
    loads[2].wait()

    def labels_in():
        lab = jnp.zeros((8, 256), F32)
        for g in range(NR):
            lab = lab + pack_r[0][g, 64:72, :]
        return jnp.concatenate([lab[0:1], lab[1:2]], axis=1).astype(jnp.int32) - 1

    def picks_in(lab, p):
        for t2 in range(5):
            t = 2 * t2 + p
            pick = jnp.where(iota((256, 512), 0) + t * 256 == lab, 1.0, 0.0).astype(BF)
            picks[p, t2 * 256 : t2 * 256 + 256, :] = pick

    def fill(k, p):
        rows = jnp.concatenate([pack_r[k][g, 0:64, :] for g in range(NR)], axis=0)
        hi, lo = split(rows)
        mine = jnp.where(c == k, 1.0, 0.0)
        got = dot1(picks[p], hi, 1, 0) + dot1(picks[p], lo, 1, 0)
        for t2 in range(5):
            part = got[t2 * 256 : t2 * 256 + 256] + hcol_ref[2 * t2 + p].astype(F32) * mine
            for h in range(2):
                p_refs[2 * k + h][p, t2] = part[:, h * 128 : (h + 1) * 128].reshape(
                    NX, NZ, 16, 128
                )

    def along_x(n):
        return (r, (n % NX) * NZ + z)

    def along_z(n):
        return (r, x * NZ + n % NZ)

    def unit(ref, g, big, n, p):
        n = n % 4
        if g % 2 == 0:
            return ref.at[p, :, n] if big else ref.at[p, :, x, n]
        return ref.at[p, :, :, n] if big else ref.at[p, :, n, z]

    def ring(g, big):
        return (x, along_x) if (g % 2 == 0) == big else (z, along_z)

    def rs(g, phase, m):
        n, dev = ring(g, phase == 0)
        buf = (first_buf, second_buf)[phase][g]
        at, p, to = (
            (n + 2, 0, n + 1), (n + 1, 1, n + 1), (n + 1, 0, n + 1),
            (n + 2, 1, n + 3), (n + 3, 0, n + 3), (n + 3, 1, n + 3),
        )[m]
        return copy(
            unit(p_refs[g], g, phase == 0, at, p), buf.at[m],
            rs_s.at[g, phase, m], rs_r.at[g, phase, m], dev(to),
        )

    def rs_start(k, phase, p):
        for m in ((0, 4), (3, 1))[p]:
            for g in (2 * k, 2 * k + 1):
                rs(g, phase, m).start()

    def rs_middle(k, phase):
        for m_in, m_out, step, p in ((0, 2, 1, 0), (3, 5, 3, 1)):
            for g in (2 * k, 2 * k + 1):
                n, dev = ring(g, phase == 0)
                rs(g, phase, m_in).wait_recv()
                ref = unit(p_refs[g], g, phase == 0, n + step, p)
                ref[...] = ref[...] + (first_buf, second_buf)[phase][g][m_in]
                rs(g, phase, m_out).start()

    def rs_end(k, phase):
        for p, (m1, m2) in enumerate(((4, 2), (1, 5))):
            for g in (2 * k, 2 * k + 1):
                n, dev = ring(g, phase == 0)
                buf = (first_buf, second_buf)[phase][g]
                rs(g, phase, m1).wait_recv()
                rs(g, phase, m2).wait_recv()
                ref = unit(p_refs[g], g, phase == 0, n, p)
                total = ref[...] + (buf[m1] + buf[m2])
                if phase == 0:
                    ref[...] = total
                else:
                    o_refs[g][p, :, x, z] = total
            if phase == 0:
                rs_start(k, 1, p)

    def ag(g, phase, m):
        n, dev = ring(g, phase == 1)
        want = (lambda i: 0) if phase == 0 else (lambda i: i % 4 // 2) if g % 2 == 0 else (lambda i: par)
        back = want(n) if phase == 1 and g % 2 == 0 else 1 - want(n)
        at, p, to = (
            (n, want(n + 1), n + 1), (n, 1 - want(n + 1), n + 1), (n, want(n + 3), n + 3),
            (n, 1 - want(n + 3), n + 3), (n + 3, want(n), n + 1), (n + 1, back, n + 3),
        )[m]
        src = unit(o_refs[g], g, phase == 1, at, p)
        return copy(src, src, ag_s.at[g, phase, m], ag_r.at[g, phase, m], dev(to))

    def ag_start(k):
        for m in (0, 3, 1, 2):
            for g in (2 * k, 2 * k + 1):
                ag(g, 0, m).start()

    def ag_forward(k):
        for m_in, m_out in ((0, 4), (3, 5)):
            for g in (2 * k, 2 * k + 1):
                ag(g, 0, m_in).wait_recv()
                ag(g, 0, m_out).start()

    def big_start(k):
        for m in (1, 2, 4, 5):
            for g in (2 * k, 2 * k + 1):
                ag(g, 0, m).wait_recv()
        for m in (0, 2):
            for g in (2 * k, 2 * k + 1):
                ag(g, 1, m).start()
        y_source(k, 0)

    def big_forward(k):
        for g in (2 * k, 2 * k + 1):
            ag(g, 1, 0).wait_recv()
            ag(g, 1, 4).start()
        for g in (2 * k, 2 * k + 1):
            ag(g, 1, 2).wait_recv()
            if g % 2 == 0:
                ag(g, 1, 5).start()
            ag(g, 1, 3).start()
            ag(g, 1, 1).start()
        y_source(k, 1)
        y_source(k, 2)

    def big_last(k):
        ag(2 * k, 1, 4).wait_recv()
        ag(2 * k, 1, 5).wait_recv()
        ag(2 * k + 1, 1, 4).wait_recv()
        y_source(k, 3)
        ag(2 * k + 1, 1, 3).wait_recv()
        ag(2 * k + 1, 1, 5).start()

    def big_end(k):
        ag(2 * k, 1, 1).wait_recv()
        ag(2 * k, 1, 3).wait_recv()
        ag(2 * k + 1, 1, 1).wait_recv()
        ag(2 * k + 1, 1, 5).wait_recv()

    y, ys = r // 2, (c % NR) // 2
    chain = side == c % 2
    hop = (y - ys + 4) % 4

    def piece(g, i):
        return ring(g, True)[0] + (0, 3, 1, 2)[i]

    def y_refs(g, i):
        n = piece(g, i) % 4
        if g % 2 == 0:
            return o_refs[g].at[par, :, n], j_refs[g].at[:, n]
        return o_refs[g].at[par, :, :, n], j_refs[g].at[:, :, n]

    def y_copy(g, i, way, from_o=False):
        o, j = y_refs(g, i)
        onward = 2 if g % 2 == 0 else 6
        to = ((r + 2) % NR, twin, (r + 6) % NR, (r + onward) % NR)[way]
        return copy(o if from_o else j, j, y_s.at[g, i, way], y_r.at[g, i], (to, c))

    def y_local(g, i):
        o, j = y_refs(g, i)
        return pltpu.make_async_copy(o, j, loc.at[g, i])

    def y_source(k, i):
        @pl.when(chain & (hop == 0))
        def _():
            for g in (2 * k, 2 * k + 1):
                for way in ((0, 2), (2, 0))[g % 2]:
                    y_copy(g, i, way, True).start()
            for g in (2 * k, 2 * k + 1):
                y_copy(g, i, 1, True).start()
                y_local(g, i).start()

    def near(k, i):
        for far in (1, 3):

            @pl.when(chain & (hop == far))
            def _():
                for g in (2 * k, 2 * k + 1) if far == 1 else (2 * k + 1, 2 * k):
                    y_copy(g, i, 1).wait_recv()
                    if (far == 1) == (g % 2 == 0):
                        y_copy(g, i, 3).start()
                    y_copy(g, i, 1).start()

    def far(k, i):
        @pl.when(chain & (hop == 2))
        def _():
            for g in (2 * k, 2 * k + 1):
                y_copy(g, i, 1).wait_recv()
                y_copy(g, i, 1).start()

    def y_last(k):
        for g in (2 * k, 2 * k + 1):
            for i in range(4):

                @pl.when(jnp.logical_not(chain))
                def _():
                    y_copy(g, i, 1).wait_recv()

                @pl.when(chain & (hop == 0))
                def _():
                    y_local(g, i).wait()
                    y_copy(g, i, 0).wait_send()
                    y_copy(g, i, 2).wait_send()

                @pl.when(chain & (hop == (1 if g % 2 == 0 else 3)))
                def _():
                    y_copy(g, i, 3).wait_send()

                @pl.when(chain)
                def _():
                    y_copy(g, i, 1).wait_send()

    done = []

    def f(count):
        for _ in range(count):
            q = len(done)
            done.append(q)
            k, part = q // 8, q % 8
            if q == 0:
                p4().wait_recv()
                build_g(
                    pv2[0].reshape(256, 256), pv2[1].reshape(256, 256),
                    pv2[2].reshape(256, 256), pat_ref[1:2, 0:1].astype(F32), g_ref,
                )
            if part == 0:
                diag_begin(k, g_ref, s_ref)
            panels(s_ref, part * 2, part * 2 + 2)
            if part == 7:
                diag_end(k, g_ref, s_ref, l_ref, v_ref)

    def e0(k):
        for d in range(1, NR):
            a2a(k, d).wait_recv()
        if k == 0:
            lab = labels_in()
        for p in (0, 1):
            if k == 0:
                picks_in(lab, p)
            fill(k, p)
            rs_start(k, 0, p)

    e0(0)
    p4_start()
    e0(1)
    f(6)
    rs_middle(0, 0)
    f(6)
    rs_end(0, 0)
    f(2)
    rs_middle(1, 0)
    f(3)
    rs_middle(0, 1)
    f(3)
    rs_end(0, 1)
    ag_start(0)
    f(3)
    ag_forward(0)
    f(2)
    rs_end(1, 0)
    f(2)
    big_start(0)
    rs_middle(1, 1)
    f(2)
    rs_end(1, 1)
    ag_start(1)
    big_forward(0)
    f(2)
    near(0, 0)
    ag_forward(1)
    f(1)
    big_start(1)
    far(0, 0)
    near(0, 1)
    big_last(0)
    near(0, 2)
    big_forward(1)
    far(0, 1)
    near(1, 0)
    near(0, 3)
    far(0, 2)
    big_last(1)
    far(0, 3)
    far(1, 0)
    near(1, 1)
    big_end(0)
    near(1, 2)
    far(1, 1)
    near(1, 3)
    far(1, 2)
    big_end(1)
    far(1, 3)
    for k in (0, 1):
        y_last(k)

    for g in range(4):
        for phase in (0, 1):
            for m in range(6):
                rs(g, phase, m).wait_send()
                ag(g, phase, m).wait_send()
    for k in (0, 1):
        for d in range(1, NR):
            a2a(k, d).wait_send()
    for b, (sr, sc) in enumerate(sources):

        @pl.when((r == sr) & (c == sc))
        def _():
            for d in range(1, NC):
                p1(b, d).wait_send()

    for k in (0, 1):

        @pl.when(r == k)
        def _():
            for d in range(1, NR):
                p2(k, d).wait_send()

    for d in range(1, NC):
        p3(d).wait_send()
    p4().wait_send()


def move(live, pattern, dest, lrow, coup, blocks):
    vm = pl.BlockSpec(memory_space=pltpu.VMEM)
    sm = pl.BlockSpec(memory_space=pltpu.SMEM)
    hb = pl.BlockSpec(memory_space=pltpu.HBM)
    dma = pltpu.SemaphoreType.DMA
    group = jax.ShapeDtypeStruct((2, 5, NX, NZ, 16, 128), F32)
    cols = jax.ShapeDtypeStruct((5, NX, NZ, 16, 128), F32)
    square = jax.ShapeDtypeStruct((512, 512), F32)
    return pl.pallas_call(
        move_kernel,
        out_shape=(group,) * 4 + (cols,) * 4 + (square, square),
        in_specs=[sm, hb, vm, vm, vm, hb],
        out_specs=[vm] * 10,
        scratch_shapes=[
            pltpu.VMEM((NR, 72, 256), F32),
            pltpu.VMEM((NR, 64, 256), F32),
            pltpu.VMEM((NR, 72, 256), F32),
            pltpu.VMEM((NR, 64, 256), F32),
            pltpu.VMEM((2, 1280, 512), BF),
            pltpu.VMEM((10, 256, 256), BF),
            pltpu.VMEM((3, NC, 16, 256), F32),
            pltpu.VMEM((3, NC, 16, 256), F32),
            pltpu.VMEM((NC, 16, 256), F32),
        ]
        + [pltpu.VMEM((2, 5, NX, NZ, 16, 128), F32)] * 4
        + [pltpu.VMEM((6, 5, 4, 16, 128), F32)] * 4
        + [pltpu.VMEM((6, 5, 16, 128), F32)] * 4
        + [
            pltpu.VMEM((512, 512), F32),
            pltpu.VMEM((128, 256), F32),
            pltpu.VMEM((80, 80), jnp.int32),
            pltpu.VMEM((256, 256), BF),
            dma((2, NR)), dma((2, NR)),
            dma((3, NC)), dma((3,)),
            dma((2, NR)), dma((2,)),
            dma((NC,)), dma((NC,)),
            dma(()), dma(()),
            dma((4, 2, 6)), dma((4, 2, 6)),
            dma((4, 2, 6)), dma((4, 2, 6)),
            dma((4, 4, 4)), dma((4, 4)),
            dma((4, 4)), dma((3,)),
        ],
        compiler_params=pltpu.CompilerParams(
            collective_id=0, has_side_effects=True, vmem_limit_bytes=40 * 1024 * 1024
        ),
        name="move",
    )(live, pattern, dest, lrow, coup, blocks)


def update_kernel(
    where_ref, pat_ref, a0_ref, a1_ref, a2_ref, a3_ref, j0_ref, j1_ref, j2_ref, j3_ref,
    l_ref, v_ref, hess_ref, o_ref, v_s, wj_s,
):
    s = pl.program_id(0)
    r, c = where_ref[0], where_ref[1]

    def wide(left, right):
        return jnp.concatenate([left, right], axis=1)

    def solve(a0, a1):
        h0, l0 = split(a0)
        h1, l1 = split(a1)
        w0 = dot1(jnp.concatenate([h0, l0, h0], 1), v_s[0:256, 0:768], 1, 1)
        w1 = dot1(jnp.concatenate([h0, l0, h0, h1, l1, h1], 1), v_s[256:512, :], 1, 1)
        return w0, w1

    @pl.when(s == 0)
    def _():
        for k in (0, 1):
            hi, lo = split(v_ref[:, k * 256 : (k + 1) * 256])
            v_s[:, k * 768 : (k + 1) * 768] = jnp.concatenate([hi, hi, lo], 1)

        def masks(k):
            out = jnp.zeros((1280, 1), F32)
            for u in range(5):
                out = jnp.where(
                    iota((1280, 1), 0) // 256 == u, pat_ref[u * NC + c, k].astype(F32), out
                )
            return out

        def tall(left, right):
            return wide(left[...].reshape(1280, 128), right[...].reshape(1280, 128))

        w0, w1 = solve(tall(j0_ref, j1_ref) * masks(0), tall(j2_ref, j3_ref) * masks(1))
        h0, l0 = split(w0)
        h1, l1 = split(w1)
        wj_s[...] = jnp.concatenate([h0, l0, h0, h1, l1, h1], 1).reshape(5, 256, 1536)

    rows = (s * 2 * NR + r, s * 2 * NR + NR + r)

    def links(k):
        return jnp.where(
            iota((512, 1), 0) < 256, pat_ref[rows[0], k], pat_ref[rows[1], k]
        ).astype(F32)

    def pair(left, right):
        return wide(left[:, s].reshape(512, 128), right[:, s].reshape(512, 128))

    w0, w1 = solve(pair(a0_ref, a1_ref) * links(0), pair(a2_ref, a3_ref) * links(1))
    h0, l0 = split(w0)
    h1, l1 = split(w1)
    wi = jnp.concatenate([h0, h0, l0, h1, h1, l1], 1)

    def put(p, u, value):
        for h in range(2):
            o_ref[pl.Slice(2560 * p + 2 * u + h, 256, 10), :] = value[:, h * 128 : (h + 1) * 128]

    for u in range(5):
        j = u * NC + c
        panel = j < 2

        @pl.when((u < s) & jnp.logical_not(panel))
        def _():
            upd = dot1(wi, wj_s[u], 1, 1)
            for p in (0, 1):
                tile = hess_ref[2 * s + p, u].astype(F32)
                put(p, u, tile * pat_ref[rows[p], j].astype(F32) - upd[p * 256 : p * 256 + 256])

        for p in (0, 1):
            i = rows[p]

            @pl.when((u == s) & (i >= j) & jnp.logical_not(panel))
            def _():
                tile = hess_ref[2 * s + p, u].astype(F32)
                upd = dot1(wi[p * 256 : p * 256 + 256], wj_s[u], 1, 1)

                @pl.when(i == j)
                def _():
                    put(p, u, sym_block(tile) - upd)

                @pl.when(i != j)
                def _():
                    put(p, u, tile * pat_ref[i, j].astype(F32) - upd)

            @pl.when((i < j) & jnp.logical_not(panel))
            def _():
                put(p, u, jnp.zeros((256, 256), F32))

            if u == 0:

                @pl.when(panel & (i >= 2))
                def _():
                    put(p, u, jnp.where(c == 0, w0, w1)[p * 256 : p * 256 + 256])

                if p == 0:

                    @pl.when(panel & (i < 2))
                    def _():
                        at = pl.ds(pl.multiple_of(i * 256, 256), 256)
                        put(p, u, jnp.where(c == 0, l_ref[at, 0:256], l_ref[at, 256:512]))


def update(where, pattern, moved, hess):
    vm = pl.BlockSpec(memory_space=pltpu.VMEM)
    sm = pl.BlockSpec(memory_space=pltpu.SMEM)
    return pl.pallas_call(
        update_kernel,
        grid=(5,),
        out_shape=jax.ShapeDtypeStruct((25600, 128), F32),
        in_specs=[sm, sm] + [vm] * 11,
        out_specs=pl.BlockSpec((5120, 128), lambda s: (s, 0)),
        scratch_shapes=[pltpu.VMEM((512, 1536), BF), pltpu.VMEM((5, 256, 1536), BF)],
        compiler_params=pltpu.CompilerParams(vmem_limit_bytes=30 * 1024 * 1024),
        name="update",
    )(
        where, pattern, *[o.reshape(2, 5, 256, 128) for o in moved[0:4]],
        *[j.reshape(5, 256, 128) for j in moved[4:8]], *moved[8:], hess,
    )


def shards(hess, coupling, dest_row, local_row, live, pattern):
    blocks = jnp.transpose(hess[:, 0, :, :, 0, :], (0, 2, 1, 3))
    where = jnp.stack([lax.axis_index("row"), lax.axis_index("col")]).astype(jnp.int32)
    coup = jnp.transpose(coupling.reshape(256, 2, 2, 128), (0, 2, 1, 3)).reshape(1024, 128)
    moved = move(
        live, pattern, dest_row.reshape(1, 256), local_row, coup, blocks
    )
    out = update(where, pattern, moved, blocks)
    return out.reshape(10, 1, 256, 5, 1, 256)


def solution(mesh):
    return jax.shard_map(
        shards,
        mesh=mesh,
        in_specs=(
            P(None, "row", None, None, "col", None),
            P(("row", "col"), None, None, None),
            P(("row", "col"), None, None),
            P(("row", "col"), None),
            P(("row", "col")),
            P(),
        ),
        out_specs=P(None, "row", None, None, "col", None),
        check_vma=False,
    )
```
